128 devices in a mesh: frames: 32 (over y, z, core), chan: 4 (over x).
Axes of the slice: x: 4, y: 4, z: 4, core: 2. Of those that a mesh axis runs over, the one named last changes fastest.
Arguments:
- spectra: float32 [2048, 64, 2048], P('frames', 'chan'), may hold values from 0.005 to 400, as said below
- chan_factor: float32 [64, 256], P('chan'), may hold values from 0.05 to 4.5, as said below
- bin_factor: float32 [2048, 256], P(('frames', 'chan')), may hold values from 0.05 to 0.5
- frame_factor: float32 [2048, 256], P('frames'), may hold values from 0.05 to 4.5, as said below
Outputs:
- chan_new: float32 [64, 256], P('chan')
- bin_new: float32 [2048, 256], P(('frames', 'chan'))
- frame_new: float32 [2048, 256], P('frames')
The draws below stay inside these ranges and needn't reach their ends.
Inputs may be any that keep to these rules, and one draw needn't show every extreme that they name: `spectra`: positive. `chan_factor`: positive. `frame_factor`: positive.
All inputs are finite; a program needn't handle non-finite values.
Results may differ from the reference program's by a relative error of at most 0.0001.
Values sent between devices are 32-bit elements; how exact they have to be, the bound alone decides.
No kernel may reach another device: no remote copies, remote signals or barrier semaphores. Data moves between devices by JAX's collectives and lax.ppermute only.
A program may use at most 64 MiB of HBM per device.

```python
import math
import jax
import jax.numpy as jnp
from jax import lax

C = 64
B = 2048
R = 256
FD = 64
F = 2048


def log_range(key, shape, lower, upper):
    return jnp.exp(jax.random.uniform(key, shape, jnp.float32, jnp.log(lower), jnp.log(upper)))


def draw_spectra(key, part):
    key = jax.random.fold_in(key, 11)
    keys = jax.random.split(key, 4)
    ramp = 3.0 ** (jnp.arange(F, dtype=jnp.float32) / F)
    frame_scale = log_range(keys[0], (F, 1, 1), 0.3, 3.0) * ramp[:, None, None]
    chan_scale = log_range(keys[1], (1, C, 1), 0.3, 3.0)
    bin_scale = log_range(keys[2], (1, 1, B), 0.3, 3.0)
    noise = log_range(keys[3], (F, C, B), 0.5, 2.0)
    return frame_scale * chan_scale * bin_scale * noise


def draw_chan_factor(key, part):
    key = jax.random.fold_in(key, 23)
    position = (jnp.arange(C, dtype=jnp.float32) / C)[:, None]
    return log_range(key, (C, R), 0.05, 0.5) * 3.0 ** position


def draw_frame_factor(key, part):
    key = jax.random.fold_in(key, 37)
    position = (jnp.arange(F, dtype=jnp.float32) / F)[:, None]
    return log_range(key, (F, R), 0.05, 0.5) * 3.0 ** position


def level_of(key, shape, shards, least, top_value):
    def one(dim, parts):
        heights = jax.random.uniform(jax.random.fold_in(jax.random.fold_in(key, 6), dim), (parts,), jnp.float32, least / len(shards), top_value / len(shards))
        return jnp.repeat(jnp.exp(heights), shape[dim] // parts).reshape((-1,) + (1,) * (len(shape) - dim - 1))

    loudness = one(*shards[0])
    for cut in shards[1:]:
        loudness = loudness * one(*cut)
    return loudness


def setup_inputs(seed: int = 0) -> dict:
    seeds = jax.random.split(jax.random.key(seed), 5)
    return {
        "spectra": draw_spectra(jax.random.fold_in(seeds[4], 71), 0),
        "chan_factor": draw_chan_factor(jax.random.fold_in(seeds[4], 71), 0),
        "bin_factor": jnp.clip(jnp.exp(math.log(0.5) - 2.3025851 * jax.random.uniform(seeds[2], (B, R), jnp.float32) ** level_of(seeds[2], (B, R), ((0, 128),), -0.2, 0.2)), 0.05, 0.5),
        "frame_factor": draw_frame_factor(jax.random.fold_in(seeds[4], 71), 0),
    }


HIGHEST_PRECISION = lax.Precision.HIGHEST


def model_block(frame_blk, chan_mat, bin_mat):
    khatri = (frame_blk[:, None, :] * chan_mat[None, :, :]).reshape(-1, chan_mat.shape[1])
    values = lax.dot_general(khatri, bin_mat, (((1,), (1,)), ((), ())), precision=HIGHEST_PRECISION, preferred_element_type=jnp.float32)
    return khatri, values


def reference(spectra, chan_factor, bin_factor, frame_factor):
    block_count = F // FD
    tensor_blocks = spectra.reshape(block_count, FD * C, B)
    frame_blocks = frame_factor.reshape(block_count, FD, R)
    col_bins = jnp.sum(bin_factor, 0)
    col_frames = jnp.sum(frame_factor, 0)

    def chan_step(running, block_pair):
        tensor_blk, frame_blk = block_pair
        khatri, values = model_block(frame_blk, chan_factor, bin_factor)
        projected = jnp.dot(tensor_blk / values, bin_factor, precision=HIGHEST_PRECISION, preferred_element_type=jnp.float32).reshape(FD, C, R)
        return running + jnp.sum(projected * frame_blk[:, None, :], 0), None

    num_chan, _ = lax.scan(chan_step, jnp.zeros((C, R), jnp.float32), (tensor_blocks, frame_blocks))
    chan_new = chan_factor * num_chan / (col_bins * col_frames)
    col_chan = jnp.sum(chan_new, 0)

    def bin_step(running, block_pair):
        tensor_blk, frame_blk = block_pair
        khatri, values = model_block(frame_blk, chan_new, bin_factor)
        ratio_vals = tensor_blk / values
        return running + lax.dot_general(ratio_vals, khatri, (((0,), (0,)), ((), ())), precision=HIGHEST_PRECISION, preferred_element_type=jnp.float32), None

    num_bins, _ = lax.scan(bin_step, jnp.zeros((B, R), jnp.float32), (tensor_blocks, frame_blocks))
    bin_new = bin_factor * num_bins / (col_chan * col_frames)
    col_bins_new = jnp.sum(bin_new, 0)

    def frame_step(block_pair):
        tensor_blk, frame_blk = block_pair
        khatri, values = model_block(frame_blk, chan_new, bin_new)
        projected = jnp.dot(tensor_blk / values, bin_new, precision=HIGHEST_PRECISION, preferred_element_type=jnp.float32).reshape(FD, C, R)
        return jnp.sum(projected * chan_new[None, :, :], 1)

    num_frames = lax.map(frame_step, (tensor_blocks, frame_blocks)).reshape(F, R)
    frame_new = frame_factor * num_frames / (col_chan * col_bins_new)
    return chan_new, bin_new, frame_new
```

```python
import jax
import jax.numpy as jnp
from jax import lax
from jax.sharding import Mesh, PartitionSpec as P

AXES = ("y", "z", "core", "x")
CHIPS = ("y", "z", "x")
SIZES = {"y": 4, "z": 4, "core": 2, "x": 4}
HIGH = lax.Precision.HIGH


def shift(value, axis, step):
    size = SIZES[axis]
    return lax.ppermute(value, axis, [(i, (i + step) % size) for i in range(size)])


def ring_sum(value, axis):
    total = value
    for step in range(1, SIZES[axis]):
        total = total + shift(value, axis, step)
    return total


def chip_exchange(value):
    return lax.all_to_all(value, CHIPS, 0, 0, tiled=True)


def gather_half(rows):
    chips = SIZES["y"] * SIZES["z"] * SIZES["x"]
    copies = jnp.broadcast_to(rows[None], (chips,) + rows.shape).reshape(-1, rows.shape[1])
    return chip_exchange(copies)


def dot(left, right, dims):
    return lax.dot_general(
        left, right, (dims, ((), ())), precision=HIGH, preferred_element_type=jnp.float32
    )


def khatri_of(frames, chans):
    return (frames[:, None, :] * chans[None, :, :]).reshape(-1, chans.shape[1])


def shards(spectra, chan_factor, bin_factor, frame_factor):
    frame_count, chan_count, bin_count = spectra.shape
    rank_count = chan_factor.shape[1]
    own_count = bin_factor.shape[0]
    half_count = bin_count // 2
    rows = spectra.reshape(frame_count * chan_count, bin_count)
    core = lax.axis_index("core")
    chip = lax.axis_index(CHIPS)

    mine = gather_half(bin_factor)
    other = shift(mine, "core", 1)
    first = jnp.where(core == 0, mine, other).reshape(16, -1, rank_count)
    second = jnp.where(core == 0, other, mine).reshape(16, -1, rank_count)
    bins_all = jnp.stack([first, second], 1).reshape(bin_count, rank_count)
    col_bins = jnp.sum(bins_all, 0)

    ratio = rows / dot(khatri_of(frame_factor, chan_factor), bins_all, ((1,), (1,)))
    projected = dot(ratio, bins_all, ((1,), (0,))).reshape(frame_count, chan_count, rank_count)
    chan_part = jnp.sum(projected * frame_factor[:, None, :], 0)
    sums = jnp.concatenate([chan_part, jnp.broadcast_to(jnp.sum(frame_factor, 0), (8, rank_count))])
    for axis in ("core", "z", "y"):
        sums = ring_sum(sums, axis)
    col_frames = sums[chan_count]
    chan_new = chan_factor * sums[:chan_count] / (col_bins * col_frames)
    col_chan = ring_sum(jnp.sum(chan_new, 0, keepdims=True), "x")[0]

    khatri = khatri_of(frame_factor, chan_new)
    ratio = rows / dot(khatri, bins_all, ((1,), (1,)))
    partial = dot(ratio, khatri, ((0,), (0,)))
    keep = lax.dynamic_slice_in_dim(partial, core * half_count, half_count, 0)
    send = lax.dynamic_slice_in_dim(partial, (1 - core) * half_count, half_count, 0)
    pieces = chip_exchange(keep + shift(send, "core", 1))
    num_bins = jnp.sum(pieces.reshape(-1, own_count, rank_count), 0)
    old = lax.dynamic_slice_in_dim(bins_all, core * half_count + chip * own_count, own_count, 0)
    piece = old * num_bins / (col_chan * col_frames)
    mine = gather_half(piece)
    other = shift(mine, "core", 1)
    first = jnp.where(core == 0, mine, other)
    second = jnp.where(core == 0, other, mine)
    bins_new = jnp.concatenate([first, second], 0)
    own = lax.axis_index(AXES)
    bins_owned = lax.dynamic_slice_in_dim(bins_new, own * own_count, own_count, 0)
    col_bins_new = jnp.sum(bins_new, 0)

    ratio = rows / dot(khatri, bins_new, ((1,), (1,)))
    projected = dot(ratio, bins_new, ((1,), (0,))).reshape(frame_count, chan_count, rank_count)
    num_frames = ring_sum(jnp.sum(projected * chan_new[None, :, :], 1), "x")
    frame_new = frame_factor * num_frames / (col_chan * col_bins_new)
    return chan_new, bins_owned, frame_new


def solution(mesh):
    split = Mesh(mesh.devices.reshape([SIZES[axis] for axis in AXES]), AXES)
    frames = ("y", "z", "core")
    in_specs = (P(frames, "x", None), P("x", None), P(AXES, None), P(frames, None))
    out_specs = (P("x", None), P(AXES, None), P(frames, None))
    return jax.shard_map(shards, mesh=split, in_specs=in_specs, out_specs=out_specs, check_vma=False)
```

```python
import functools
import math

import jax
import jax.numpy as jnp
from jax import lax
from jax.experimental import pallas as pl
from jax.experimental.pallas import tpu as pltpu
from jax.sharding import Mesh, PartitionSpec as P

AXES = ("y", "z", "core", "x")
CHIPS = ("y", "z", "x")
PLANE = ("y", "z")
SIZES = {"y": 4, "z": 4, "core": 2, "x": 4}
F32 = jnp.float32
BF16 = jnp.bfloat16
NT = (((1,), (1,)), ((), ()))
NN = (((1,), (0,)), ((), ()))
VMEM = pl.BlockSpec(memory_space=pltpu.VMEM)
TILE = 512
CHUNK = 256


def shift(value, axis, step):
    size = SIZES[axis]
    return lax.ppermute(value, axis, [(i, (i + step) % size) for i in range(size)])


def ring_sum(value, axis):
    total = value
    for step in range(1, SIZES[axis]):
        total = total + shift(value, axis, step)
    return total


def exchange(value, axes):
    return lax.all_to_all(value, axes, 0, 0, tiled=True)


def gather(rows, axes):
    count = math.prod(SIZES[axis] for axis in axes)
    copies = jnp.broadcast_to(rows[None], (count,) + rows.shape).reshape(-1, rows.shape[1])
    return exchange(copies, axes)


def split(value):
    high = value.astype(BF16)
    return high, (value - high.astype(F32)).astype(BF16)


def triple(value, axis, order):
    high, low = split(value)
    parts = {"h": high, "l": low}
    return jnp.concatenate([parts[part] for part in order], axis)


def product(left, right, dims):
    return lax.dot_general(left, right, dims, preferred_element_type=F32)


def khatri_of(frames, chans):
    return (frames[:, None, :] * chans[None, :, :]).reshape(-1, chans.shape[1])


def half_lanes(x_ref, rows, start, count, parity):
    lane = lax.broadcasted_iota(jnp.int32, (CHUNK, 128), 1)
    lower = lane < 64
    keep = lower == (parity == 0)
    pieces = []
    for at in range(2 * start, 2 * (start + count), 256):
        first = x_ref[rows, at : at + 128]
        second = x_ref[rows, at + 128 : at + 256]
        straight = jnp.where(lower, first, second)
        crossed = pltpu.roll(jnp.where(lower, second, first), 64, 1)
        pieces.append(jnp.where(keep, straight, crossed))
    return jnp.concatenate(pieces, 1)


def ratio_of(x_ref, khatri_ref, rows, start, count, parity, bins_right):
    model = product(khatri_ref[rows, :], bins_right, NT)
    guess = pl.reciprocal(model, approx=True)
    inverse = guess * (2.0 - model * guess)
    return half_lanes(x_ref, rows, start, count, parity) * inverse


def parity_of(mine):
    core = lax.axis_index("core")
    return core if mine else 1 - core


def row_sums(value):
    return jnp.sum(value.reshape(-1, 8, value.shape[1]), 0)


def project_kernel(over, mine, x_ref, frames_ref, chans_ref, bins_ref, *rest):
    before_ref = None
    if len(rest) == 5:
        before_ref, rest = rest[0], rest[1:]
    out_ref, cols_ref, khatri_ref, total_ref = rest
    frames, chans = frames_ref[...], chans_ref[...]
    parity = parity_of(mine)
    khatri_ref[...] = triple(khatri_of(frames, chans), 1, "hlh")
    count = bins_ref.shape[0]
    for start in range(0, count, TILE):
        bins = bins_ref[start : start + TILE, :]
        bins_right = triple(bins, 1, "hhl")
        bins_down = triple(bins, 0, "hhl")
        for at in range(0, x_ref.shape[0], CHUNK):
            rows = pl.ds(at, CHUNK)
            ratio = ratio_of(x_ref, khatri_ref, rows, start, TILE, parity, bins_right)
            part = product(triple(ratio, 1, "hlh"), bins_down, NN)
            total_ref[rows, :] = part if start == 0 else total_ref[rows, :] + part
    projected = total_ref[...].reshape(frames.shape[0], chans.shape[0], -1)
    if over == "frames":
        result = jnp.sum(projected * frames[:, None, :], 0)
    else:
        result = jnp.sum(projected * chans[None, :, :], 1)
    size = result.shape[0]
    if before_ref is not None:
        result = result + before_ref[:size, :]
    out_ref[:size, :] = result
    if over == "frames":
        out_ref[size:, :] = row_sums(frames)
    cols_ref[...] = row_sums(bins_ref[...])


def spread_kernel(mine, x_ref, frames_ref, chans_ref, bins_ref, out_ref, khatri_ref, turned_ref):
    parity = parity_of(mine)
    khatri = khatri_of(frames_ref[...], chans_ref[...])
    khatri_ref[...] = triple(khatri, 1, "hlh")
    high, low = split(khatri.T)
    turned_ref[0] = high
    turned_ref[1] = low
    count = bins_ref.shape[0]
    for start in range(0, count, TILE):
        bins_right = triple(bins_ref[start : start + TILE, :], 1, "hhl")
        total = None
        for at in range(0, x_ref.shape[0], CHUNK):
            rows = pl.ds(at, CHUNK)
            ratio = ratio_of(x_ref, khatri_ref, rows, start, TILE, parity, bins_right)
            left = jnp.concatenate([turned_ref[0, :, rows], turned_ref[0, :, rows], turned_ref[1, :, rows]], 1)
            part = product(left, triple(ratio, 0, "hlh"), NN)
            total = part if total is None else total + part
        out_ref[start : start + TILE, :] = total.T


def call(kernel, out_shape, scratch, x, frames, chans, bins, *more, name):
    rows, count, rank = x.shape[0], bins.shape[0], bins.shape[1]
    return pl.pallas_call(
        kernel,
        in_specs=[VMEM] * (4 + len(more)),
        out_specs=jax.tree.map(lambda _: VMEM, out_shape),
        out_shape=out_shape,
        scratch_shapes=scratch,
        compiler_params=pltpu.CompilerParams(vmem_limit_bytes=8 << 20),
        cost_estimate=pl.CostEstimate(
            flops=12 * rows * count * rank, bytes_accessed=4 * (rows + rank) * count, transcendentals=rows * count
        ),
        name=name,
    )(x, frames, chans, bins, *more)


def project(over, mine, x, frames, chans, bins, *before):
    rank = bins.shape[1]
    out_rows = chans.shape[0] + 8 if over == "frames" else frames.shape[0]
    out_shape = (jax.ShapeDtypeStruct((out_rows, rank), F32), jax.ShapeDtypeStruct((8, rank), F32))
    scratch = [pltpu.VMEM((x.shape[0], 3 * rank), BF16), pltpu.VMEM((x.shape[0], rank), F32)]
    kernel = functools.partial(project_kernel, over, mine)
    return call(kernel, out_shape, scratch, x, frames, chans, bins, *before, name="project")


def spread(mine, x, frames, chans, bins):
    rank = bins.shape[1]
    out_shape = jax.ShapeDtypeStruct(bins.shape, F32)
    scratch = [pltpu.VMEM((x.shape[0], 3 * rank), BF16), pltpu.VMEM((2, rank, x.shape[0]), BF16)]
    return call(functools.partial(spread_kernel, mine), out_shape, scratch, x, frames, chans, bins, name="spread")


def renew_kernel(sums_ref, bins_ref, col_frames_ref, line_ref, own_ref, col_chan_ref):
    line_count, own_count = bins_ref.shape[0] // (SIZES["y"] * SIZES["z"]), own_ref.shape[0]
    place = lax.axis_index("y") * SIZES["z"] + lax.axis_index("z")
    col_chan = sums_ref[line_count : line_count + 1, :]
    scale = 1.0 / (col_chan * col_frames_ref[...])
    old = bins_ref[pl.ds(pl.multiple_of(place * line_count, line_count), line_count), :]
    new = old * sums_ref[:line_count, :] * scale
    for at in range(0, line_ref.shape[0], line_count):
        line_ref[at : at + line_count, :] = new
    start = pl.multiple_of(lax.axis_index("x") * own_count, own_count)
    own_ref[...] = line_ref[pl.ds(start, own_count), :]
    col_chan_ref[...] = col_chan


def renew(sums, bins, col_frames, own_count):
    rank = bins.shape[1]
    shapes = (bins.shape, (own_count, rank), (1, rank))
    return pl.pallas_call(
        renew_kernel,
        in_specs=[VMEM] * 3,
        out_specs=[VMEM] * 3,
        out_shape=[jax.ShapeDtypeStruct(shape, F32) for shape in shapes],
        compiler_params=pltpu.CompilerParams(vmem_limit_bytes=8 << 20),
        name="renew",
    )(sums, bins, col_frames)


def shards(spectra, chan_factor, bin_factor, frame_factor):
    frame_count, chan_count, bin_count = spectra.shape
    rank_count = chan_factor.shape[1]
    own_count = bin_factor.shape[0]
    x = spectra.reshape(frame_count * chan_count, bin_count)

    bins_mine = gather(bin_factor, CHIPS)
    bins_other = shift(bins_mine, "core", 1)
    sums, cols_mine = project("frames", True, x, frame_factor, chan_factor, bins_mine)
    sums, cols_other = project("frames", False, x, frame_factor, chan_factor, bins_other, sums)
    col_bins = jnp.sum(cols_mine + cols_other, 0)
    for axis in ("core", "z", "y"):
        sums = ring_sum(sums, axis)
    col_frames = jnp.sum(sums[chan_count:], 0, keepdims=True)
    chan_new = chan_factor * sums[:chan_count] / (col_bins * col_frames)

    part_other = spread(False, x, frame_factor, chan_new, bins_other)
    arrived = shift(part_other, "core", 1)
    part_mine = spread(True, x, frame_factor, chan_new, bins_mine)
    line_count = own_count * SIZES["x"]
    pieces = exchange(part_mine + arrived, PLANE).reshape(-1, line_count, rank_count)
    cols = jnp.broadcast_to(jnp.sum(chan_new, 0), (8, rank_count))
    sums = ring_sum(jnp.concatenate([jnp.sum(pieces, 0), cols]), "x")
    line_bins, bin_new, col_chan = renew(sums, bins_mine, col_frames, own_count)

    bins_mine = exchange(line_bins, PLANE)
    bins_other = shift(bins_mine, "core", 1)
    part, cols_mine = project("chans", True, x, frame_factor, chan_new, bins_mine)
    part, cols_other = project("chans", False, x, frame_factor, chan_new, bins_other, part)
    col_bins_new = jnp.sum(cols_mine + cols_other, 0)
    frame_new = frame_factor * ring_sum(part, "x") / (col_chan * col_bins_new)
    return chan_new, bin_new, frame_new


def solution(mesh):
    split_mesh = Mesh(mesh.devices.reshape([SIZES[axis] for axis in AXES]), AXES)
    frames = ("y", "z", "core")
    in_specs = (P(frames, "x", None), P("x", None), P(AXES, None), P(frames, None))
    out_specs = (P("x", None), P(AXES, None), P(frames, None))
    return jax.shard_map(shards, mesh=split_mesh, in_specs=in_specs, out_specs=out_specs, check_vma=False)
```

```python
import functools
import math

import jax
import jax.numpy as jnp
from jax import lax
from jax.experimental import pallas as pl
from jax.experimental.pallas import tpu as pltpu
from jax.sharding import Mesh, PartitionSpec as P

AXES = ("y", "z", "core", "x")
CHIPS = ("y", "z", "x")
PLANE = ("y", "z")
SIZES = {"y": 4, "z": 4, "core": 2, "x": 4}
F32 = jnp.float32
BF16 = jnp.bfloat16
NT = (((1,), (1,)), ((), ()))
NN = (((1,), (0,)), ((), ()))
VMEM = pl.BlockSpec(memory_space=pltpu.VMEM)
TILE = 512
CHUNK = 256
WIDE = 512


def shift(value, axis, step):
    size = SIZES[axis]
    return lax.ppermute(value, axis, [(i, (i + step) % size) for i in range(size)])


def ring_sum(value, axis):
    total = value
    for step in range(1, SIZES[axis]):
        total = total + shift(value, axis, step)
    return total


def exchange(value, axes):
    return lax.all_to_all(value, axes, 0, 0, tiled=True)


def split(value):
    high = value.astype(BF16)
    return high, (value - high.astype(F32)).astype(BF16)


def triple(value, axis, order):
    high, low = split(value)
    parts = {"h": high, "l": low}
    return jnp.concatenate([parts[part] for part in order], axis)


def product(left, right, dims):
    return lax.dot_general(left, right, dims, preferred_element_type=F32)


def khatri_of(frames, chans):
    return (frames[:, None, :] * chans[None, :, :]).reshape(-1, chans.shape[1])


def half_lanes(x_ref, rows, start, count, parity):
    lane = lax.broadcasted_iota(jnp.int32, (rows.size, 128), 1)
    lower = lane < 64
    keep = lower == (parity == 0)
    pieces = []
    for at in range(2 * start, 2 * (start + count), 256):
        first = x_ref[rows, at : at + 128]
        second = x_ref[rows, at + 128 : at + 256]
        straight = jnp.where(lower, first, second)
        crossed = pltpu.roll(jnp.where(lower, second, first), 64, 1)
        pieces.append(jnp.where(keep, straight, crossed))
    return jnp.concatenate(pieces, 1)


def ratio_of(x_ref, khatri_ref, rows, start, count, parity, bins_right):
    model = product(khatri_ref[rows, :], bins_right, NT)
    guess = pl.reciprocal(model, approx=True)
    inverse = guess * (2.0 - model * guess)
    return half_lanes(x_ref, rows, start, count, parity) * inverse


def parity_of(mine):
    core = lax.axis_index("core")
    return core if mine else 1 - core


def row_sums(value):
    return jnp.sum(value.reshape(-1, 8, value.shape[1]), 0)


def project_kernel(over, mine, x_ref, frames_ref, chans_ref, bins_ref, *rest):
    before_ref = None
    if len(rest) == 5:
        before_ref, rest = rest[0], rest[1:]
    out_ref, cols_ref, khatri_ref, total_ref = rest
    frames, chans = frames_ref[...], chans_ref[...]
    parity = parity_of(mine)
    khatri_ref[...] = triple(khatri_of(frames, chans), 1, "hlh")
    count = bins_ref.shape[0]
    for start in range(0, count, TILE):
        bins = bins_ref[start : start + TILE, :]
        bins_right = triple(bins, 1, "hhl")
        bins_down = triple(bins, 0, "hhl")
        for at in range(0, x_ref.shape[0], CHUNK):
            rows = pl.ds(at, CHUNK)
            ratio = ratio_of(x_ref, khatri_ref, rows, start, TILE, parity, bins_right)
            part = product(triple(ratio, 1, "hlh"), bins_down, NN)
            total_ref[rows, :] = part if start == 0 else total_ref[rows, :] + part
    projected = total_ref[...].reshape(frames.shape[0], chans.shape[0], -1)
    if over == "frames":
        result = jnp.sum(projected * frames[:, None, :], 0)
    else:
        result = jnp.sum(projected * chans[None, :, :], 1)
    size = result.shape[0]
    if before_ref is not None:
        result = result + before_ref[:size, :]
    out_ref[:size, :] = result
    if over == "frames":
        out_ref[size:, :] = row_sums(frames)
    cols_ref[...] = row_sums(bins_ref[...])


def spread_kernel(mine, x_ref, frames_ref, chans_ref, bins_ref, out_ref, khatri_ref, turned_ref):
    parity = parity_of(mine)
    khatri = khatri_of(frames_ref[...], chans_ref[...])
    khatri_ref[...] = triple(khatri, 1, "hlh")
    high, low = split(khatri.T)
    turned_ref[0] = high
    turned_ref[1] = low
    count = bins_ref.shape[0]
    for start in range(0, count, TILE):
        bins_right = triple(bins_ref[start : start + TILE, :], 1, "hhl")
        total = None
        for at in range(0, x_ref.shape[0], WIDE):
            rows = pl.ds(at, WIDE)
            ratio = ratio_of(x_ref, khatri_ref, rows, start, TILE, parity, bins_right)
            left = jnp.concatenate([turned_ref[0, :, rows], turned_ref[0, :, rows], turned_ref[1, :, rows]], 1)
            part = product(left, triple(ratio, 0, "hlh"), NN)
            total = part if total is None else total + part
        out_ref[start : start + TILE, :] = total.T


def call(kernel, out_shape, scratch, x, frames, chans, bins, *more, limit=8, name):
    rows, count, rank = x.shape[0], bins.shape[0], bins.shape[1]
    return pl.pallas_call(
        kernel,
        in_specs=[VMEM] * (4 + len(more)),
        out_specs=jax.tree.map(lambda _: VMEM, out_shape),
        out_shape=out_shape,
        scratch_shapes=scratch,
        compiler_params=pltpu.CompilerParams(vmem_limit_bytes=limit << 20),
        cost_estimate=pl.CostEstimate(
            flops=12 * rows * count * rank, bytes_accessed=4 * (rows + rank) * count, transcendentals=rows * count
        ),
        name=name,
    )(x, frames, chans, bins, *more)


def project(over, mine, x, frames, chans, bins, *before):
    rank = bins.shape[1]
    out_rows = chans.shape[0] + 8 if over == "frames" else frames.shape[0]
    out_shape = (jax.ShapeDtypeStruct((out_rows, rank), F32), jax.ShapeDtypeStruct((8, rank), F32))
    scratch = [pltpu.VMEM((x.shape[0], 3 * rank), BF16), pltpu.VMEM((x.shape[0], rank), F32)]
    kernel = functools.partial(project_kernel, over, mine)
    return call(kernel, out_shape, scratch, x, frames, chans, bins, *before, name="project")


def spread(mine, x, frames, chans, bins):
    rank = bins.shape[1]
    out_shape = jax.ShapeDtypeStruct(bins.shape, F32)
    scratch = [pltpu.VMEM((x.shape[0], 3 * rank), BF16), pltpu.VMEM((2, rank, x.shape[0]), BF16)]
    return call(functools.partial(spread_kernel, mine), out_shape, scratch, x, frames, chans, bins, limit=16, name="spread")


LONG = pl.CostEstimate(flops=30_000_000_000, bytes_accessed=0, transcendentals=0)


def copies_kernel(rows_ref, out_ref):
    rows = rows_ref[...]
    for at in range(0, out_ref.shape[0], rows.shape[0]):
        out_ref[at : at + rows.shape[0], :] = rows


def copies(rows, count):
    return pl.pallas_call(
        copies_kernel,
        in_specs=[VMEM],
        out_specs=VMEM,
        out_shape=jax.ShapeDtypeStruct((rows.shape[0] * count, rows.shape[1]), F32),
        compiler_params=pltpu.CompilerParams(vmem_limit_bytes=8 << 20),
        cost_estimate=LONG,
        name="copies",
    )(rows)


def collect_kernel(pieces_ref, chans_ref, out_ref):
    size = out_ref.shape[0] - 8
    total = pieces_ref[:size, :]
    for at in range(size, pieces_ref.shape[0], size):
        total = total + pieces_ref[at : at + size, :]
    out_ref[:size, :] = total
    out_ref[size:, :] = jnp.broadcast_to(jnp.sum(chans_ref[...], 0, keepdims=True), (8, out_ref.shape[1]))


def collect(pieces, chans, line_count):
    return pl.pallas_call(
        collect_kernel,
        in_specs=[VMEM] * 2,
        out_specs=VMEM,
        out_shape=jax.ShapeDtypeStruct((line_count + 8, pieces.shape[1]), F32),
        compiler_params=pltpu.CompilerParams(vmem_limit_bytes=8 << 20),
        name="collect",
    )(pieces, chans)


def renew_kernel(sums_ref, bins_ref, col_frames_ref, line_ref, own_ref, col_chan_ref):
    line_count, own_count = bins_ref.shape[0] // (SIZES["y"] * SIZES["z"]), own_ref.shape[0]
    place = lax.axis_index("y") * SIZES["z"] + lax.axis_index("z")
    col_chan = sums_ref[line_count : line_count + 1, :]
    scale = 1.0 / (col_chan * col_frames_ref[...])
    old = bins_ref[pl.ds(pl.multiple_of(place * line_count, line_count), line_count), :]
    new = old * sums_ref[:line_count, :] * scale
    for at in range(0, line_ref.shape[0], line_count):
        line_ref[at : at + line_count, :] = new
    start = pl.multiple_of(lax.axis_index("x") * own_count, own_count)
    own_ref[...] = line_ref[pl.ds(start, own_count), :]
    col_chan_ref[...] = col_chan


def renew(sums, bins, col_frames, own_count):
    rank = bins.shape[1]
    shapes = (bins.shape, (own_count, rank), (1, rank))
    return pl.pallas_call(
        renew_kernel,
        in_specs=[VMEM] * 3,
        out_specs=[VMEM] * 3,
        out_shape=[jax.ShapeDtypeStruct(shape, F32) for shape in shapes],
        compiler_params=pltpu.CompilerParams(vmem_limit_bytes=8 << 20),
        cost_estimate=LONG,
        name="renew",
    )(sums, bins, col_frames)


def shards(spectra, chan_factor, bin_factor, frame_factor):
    frame_count, chan_count, bin_count = spectra.shape
    rank_count = chan_factor.shape[1]
    own_count = bin_factor.shape[0]
    x = spectra.reshape(frame_count * chan_count, bin_count)

    bins_mine = exchange(copies(bin_factor, math.prod(SIZES[axis] for axis in CHIPS)), CHIPS)
    bins_other = shift(bins_mine, "core", 1)
    sums, cols_mine = project("frames", True, x, frame_factor, chan_factor, bins_mine)
    sums, cols_other = project("frames", False, x, frame_factor, chan_factor, bins_other, sums)
    col_bins = jnp.sum(cols_mine + cols_other, 0)
    for axis in ("core", "z", "y"):
        sums = ring_sum(sums, axis)
    col_frames = jnp.sum(sums[chan_count:], 0, keepdims=True)
    chan_new = chan_factor * sums[:chan_count] / (col_bins * col_frames)

    part_other = spread(False, x, frame_factor, chan_new, bins_other)
    arrived = shift(part_other, "core", 1)
    part_mine = spread(True, x, frame_factor, chan_new, bins_mine)
    line_count = own_count * SIZES["x"]
    pieces = exchange(part_mine + arrived, PLANE)
    sums = ring_sum(collect(pieces, chan_new, line_count), "x")
    line_bins, bin_new, col_chan = renew(sums, bins_mine, col_frames, own_count)

    bins_mine = exchange(line_bins, PLANE)
    bins_other = shift(bins_mine, "core", 1)
    part, cols_mine = project("chans", True, x, frame_factor, chan_new, bins_mine)
    part, cols_other = project("chans", False, x, frame_factor, chan_new, bins_other, part)
    col_bins_new = jnp.sum(cols_mine + cols_other, 0)
    frame_new = frame_factor * ring_sum(part, "x") / (col_chan * col_bins_new)
    return chan_new, bin_new, frame_new


def solution(mesh):
    split_mesh = Mesh(mesh.devices.reshape([SIZES[axis] for axis in AXES]), AXES)
    frames = ("y", "z", "core")
    in_specs = (P(frames, "x", None), P("x", None), P(AXES, None), P(frames, None))
    out_specs = (P("x", None), P(AXES, None), P(frames, None))
    return jax.shard_map(shards, mesh=split_mesh, in_specs=in_specs, out_specs=out_specs, check_vma=False)
```

```python
import functools
import math

import jax
import jax.numpy as jnp
from jax import lax
from jax.experimental import pallas as pl
from jax.experimental.pallas import tpu as pltpu
from jax.sharding import Mesh, PartitionSpec as P

AXES = ("y", "z", "core", "x")
CHIPS = ("y", "z", "x")
PLANE = ("y", "z")
SIZES = {"y": 4, "z": 4, "core": 2, "x": 4}
F32 = jnp.float32
BF16 = jnp.bfloat16
NT = (((1,), (1,)), ((), ()))
NN = (((1,), (0,)), ((), ()))
VMEM = pl.BlockSpec(memory_space=pltpu.VMEM)
TILE = 512
CHUNK = 256
WIDE = 512


def shift(value, axis, step):
    size = SIZES[axis]
    return lax.ppermute(value, axis, [(i, (i + step) % size) for i in range(size)])


def ring_sum(value, axis):
    total = value
    for step in range(1, SIZES[axis]):
        total = total + shift(value, axis, step)
    return total


def exchange(value, axes):
    return lax.all_to_all(value, axes, 0, 0, tiled=True)


def split(value):
    high = value.astype(BF16)
    return high, (value - high.astype(F32)).astype(BF16)


def triple(value, axis, order):
    high, low = split(value)
    parts = {"h": high, "l": low}
    return jnp.concatenate([parts[part] for part in order], axis)


def product(left, right, dims):
    return lax.dot_general(left, right, dims, preferred_element_type=F32)


def khatri_of(frames, chans):
    return (frames[:, None, :] * chans[None, :, :]).reshape(-1, chans.shape[1])


def half_lanes(x_ref, rows, start, count, parity):
    lane = lax.broadcasted_iota(jnp.int32, (rows.size, 128), 1)
    lower = lane < 64
    keep = lower == (parity == 0)
    pieces = []
    for at in range(2 * start, 2 * (start + count), 256):
        first = x_ref[rows, at : at + 128]
        second = x_ref[rows, at + 128 : at + 256]
        straight = jnp.where(lower, first, second)
        crossed = pltpu.roll(jnp.where(lower, second, first), 64, 1)
        pieces.append(jnp.where(keep, straight, crossed))
    return jnp.concatenate(pieces, 1)


def ratio_of(x_ref, khatri_ref, rows, start, count, parity, bins_right):
    model = product(khatri_ref[rows, :], bins_right, NT)
    guess = pl.reciprocal(model, approx=True)
    inverse = guess * (2.0 - model * guess)
    return half_lanes(x_ref, rows, start, count, parity) * inverse


def parity_of(mine):
    core = lax.axis_index("core")
    return core if mine else 1 - core


def row_sums(value):
    return jnp.sum(value.reshape(-1, 8, value.shape[1]), 0)


def project_kernel(over, mine, x_ref, frames_ref, chans_ref, bins_ref, *rest):
    before_ref = None
    if len(rest) == 5:
        before_ref, rest = rest[0], rest[1:]
    out_ref, cols_ref, khatri_ref, total_ref = rest
    frames, chans = frames_ref[...], chans_ref[...]
    parity = parity_of(mine)
    khatri_ref[...] = triple(khatri_of(frames, chans), 1, "hlh")
    count = bins_ref.shape[0]
    for start in range(0, count, TILE):
        bins = bins_ref[start : start + TILE, :]
        bins_right = triple(bins, 1, "hhl")
        bins_down = triple(bins, 0, "hhl")
        for at in range(0, x_ref.shape[0], CHUNK):
            rows = pl.ds(at, CHUNK)
            ratio = ratio_of(x_ref, khatri_ref, rows, start, TILE, parity, bins_right)
            part = product(triple(ratio, 1, "hlh"), bins_down, NN)
            total_ref[rows, :] = part if start == 0 else total_ref[rows, :] + part
    projected = total_ref[...].reshape(frames.shape[0], chans.shape[0], -1)
    if over == "frames":
        result = jnp.sum(projected * frames[:, None, :], 0)
    else:
        result = jnp.sum(projected * chans[None, :, :], 1)
    size = result.shape[0]
    if before_ref is not None:
        result = result + before_ref[:size, :]
    if over == "frames":
        result = jnp.concatenate([result, row_sums(frames)], 0)
    for at in range(0, out_ref.shape[0], result.shape[0]):
        out_ref[at : at + result.shape[0], :] = result
    cols_ref[...] = row_sums(bins_ref[...])


def spread_kernel(mine, x_ref, frames_ref, chans_ref, bins_ref, out_ref, khatri_ref, turned_ref):
    parity = parity_of(mine)
    khatri = khatri_of(frames_ref[...], chans_ref[...])
    khatri_ref[...] = triple(khatri, 1, "hlh")
    high, low = split(khatri.T)
    turned_ref[0] = high
    turned_ref[1] = low
    count = bins_ref.shape[0]
    for start in range(0, count, TILE):
        bins_right = triple(bins_ref[start : start + TILE, :], 1, "hhl")
        total = None
        for at in range(0, x_ref.shape[0], WIDE):
            rows = pl.ds(at, WIDE)
            ratio = ratio_of(x_ref, khatri_ref, rows, start, TILE, parity, bins_right)
            left = jnp.concatenate([turned_ref[0, :, rows], turned_ref[0, :, rows], turned_ref[1, :, rows]], 1)
            part = product(left, triple(ratio, 0, "hlh"), NN)
            total = part if total is None else total + part
        out_ref[start : start + TILE, :] = total.T


def call(kernel, out_shape, scratch, x, frames, chans, bins, *more, limit=8, name):
    rows, count, rank = x.shape[0], bins.shape[0], bins.shape[1]
    return pl.pallas_call(
        kernel,
        in_specs=[VMEM] * (4 + len(more)),
        out_specs=jax.tree.map(lambda _: VMEM, out_shape),
        out_shape=out_shape,
        scratch_shapes=scratch,
        compiler_params=pltpu.CompilerParams(vmem_limit_bytes=limit << 20),
        cost_estimate=pl.CostEstimate(
            flops=12 * rows * count * rank, bytes_accessed=4 * (rows + rank) * count, transcendentals=rows * count
        ),
        name=name,
    )(x, frames, chans, bins, *more)


def project(over, mine, x, frames, chans, bins, *before, count=1):
    rank = bins.shape[1]
    out_rows = count * (chans.shape[0] + 8 if over == "frames" else frames.shape[0])
    out_shape = (jax.ShapeDtypeStruct((out_rows, rank), F32), jax.ShapeDtypeStruct((8, rank), F32))
    scratch = [pltpu.VMEM((x.shape[0], 3 * rank), BF16), pltpu.VMEM((x.shape[0], rank), F32)]
    kernel = functools.partial(project_kernel, over, mine)
    return call(kernel, out_shape, scratch, x, frames, chans, bins, *before, name="project")


def spread(mine, x, frames, chans, bins):
    rank = bins.shape[1]
    out_shape = jax.ShapeDtypeStruct(bins.shape, F32)
    scratch = [pltpu.VMEM((x.shape[0], 3 * rank), BF16), pltpu.VMEM((2, rank, x.shape[0]), BF16)]
    return call(functools.partial(spread_kernel, mine), out_shape, scratch, x, frames, chans, bins, limit=16, name="spread")


LONG = pl.CostEstimate(flops=30_000_000_000, bytes_accessed=0, transcendentals=0)


def copies_kernel(rows_ref, out_ref):
    rows = rows_ref[...]
    for at in range(0, out_ref.shape[0], rows.shape[0]):
        out_ref[at : at + rows.shape[0], :] = rows


def copies(rows, count):
    return pl.pallas_call(
        copies_kernel,
        in_specs=[VMEM],
        out_specs=VMEM,
        out_shape=jax.ShapeDtypeStruct((rows.shape[0] * count, rows.shape[1]), F32),
        compiler_params=pltpu.CompilerParams(vmem_limit_bytes=8 << 20),
        cost_estimate=LONG,
        name="copies",
    )(rows)


def collect_kernel(pieces_ref, chans_ref, out_ref):
    size = out_ref.shape[0] - 8
    total = pieces_ref[:size, :]
    for at in range(size, pieces_ref.shape[0], size):
        total = total + pieces_ref[at : at + size, :]
    out_ref[:size, :] = total
    out_ref[size:, :] = jnp.broadcast_to(jnp.sum(chans_ref[...], 0, keepdims=True), (8, out_ref.shape[1]))


def collect(pieces, chans, line_count):
    return pl.pallas_call(
        collect_kernel,
        in_specs=[VMEM] * 2,
        out_specs=VMEM,
        out_shape=jax.ShapeDtypeStruct((line_count + 8, pieces.shape[1]), F32),
        compiler_params=pltpu.CompilerParams(vmem_limit_bytes=8 << 20),
        name="collect",
    )(pieces, chans)


def fold_kernel(pieces_ref, out_ref):
    size = out_ref.shape[0]
    total = pieces_ref[:size, :]
    for at in range(size, pieces_ref.shape[0], size):
        total = total + pieces_ref[at : at + size, :]
    out_ref[...] = total


def fold(pieces, size):
    return pl.pallas_call(
        fold_kernel,
        in_specs=[VMEM],
        out_specs=VMEM,
        out_shape=jax.ShapeDtypeStruct((size, pieces.shape[1]), F32),
        compiler_params=pltpu.CompilerParams(vmem_limit_bytes=8 << 20),
        name="fold",
    )(pieces)


def renew_kernel(sums_ref, bins_ref, col_frames_ref, line_ref, own_ref, col_chan_ref):
    line_count, own_count = bins_ref.shape[0] // (SIZES["y"] * SIZES["z"]), own_ref.shape[0]
    place = lax.axis_index("y") * SIZES["z"] + lax.axis_index("z")
    col_chan = sums_ref[line_count : line_count + 1, :]
    scale = 1.0 / (col_chan * col_frames_ref[...])
    old = bins_ref[pl.ds(pl.multiple_of(place * line_count, line_count), line_count), :]
    new = old * sums_ref[:line_count, :] * scale
    for at in range(0, line_ref.shape[0], line_count):
        line_ref[at : at + line_count, :] = new
    start = pl.multiple_of(lax.axis_index("x") * own_count, own_count)
    own_ref[...] = line_ref[pl.ds(start, own_count), :]
    col_chan_ref[...] = col_chan


def renew(sums, bins, col_frames, own_count):
    rank = bins.shape[1]
    shapes = (bins.shape, (own_count, rank), (1, rank))
    return pl.pallas_call(
        renew_kernel,
        in_specs=[VMEM] * 3,
        out_specs=[VMEM] * 3,
        out_shape=[jax.ShapeDtypeStruct(shape, F32) for shape in shapes],
        compiler_params=pltpu.CompilerParams(vmem_limit_bytes=8 << 20),
        cost_estimate=LONG,
        name="renew",
    )(sums, bins, col_frames)


def shards(spectra, chan_factor, bin_factor, frame_factor):
    frame_count, chan_count, bin_count = spectra.shape
    rank_count = chan_factor.shape[1]
    own_count = bin_factor.shape[0]
    x = spectra.reshape(frame_count * chan_count, bin_count)

    bins_mine = exchange(copies(bin_factor, math.prod(SIZES[axis] for axis in CHIPS)), CHIPS)
    bins_other = shift(bins_mine, "core", 1)
    sums, cols_mine = project("frames", True, x, frame_factor, chan_factor, bins_mine)
    places = SIZES["y"] * SIZES["z"]
    sums, cols_other = project("frames", False, x, frame_factor, chan_factor, bins_other, sums, count=places)
    col_bins = jnp.sum(cols_mine + cols_other, 0)
    sums = ring_sum(fold(exchange(sums, PLANE), sums.shape[0] // places), "core")
    col_frames = jnp.sum(sums[chan_count:], 0, keepdims=True)
    chan_new = chan_factor * sums[:chan_count] / (col_bins * col_frames)

    part_other = spread(False, x, frame_factor, chan_new, bins_other)
    arrived = shift(part_other, "core", 1)
    part_mine = spread(True, x, frame_factor, chan_new, bins_mine)
    line_count = own_count * SIZES["x"]
    pieces = exchange(part_mine + arrived, PLANE)
    sums = ring_sum(collect(pieces, chan_new, line_count), "x")
    line_bins, bin_new, col_chan = renew(sums, bins_mine, col_frames, own_count)

    bins_mine = exchange(line_bins, PLANE)
    bins_other = shift(bins_mine, "core", 1)
    part, cols_mine = project("chans", True, x, frame_factor, chan_new, bins_mine)
    part, cols_other = project("chans", False, x, frame_factor, chan_new, bins_other, part)
    col_bins_new = jnp.sum(cols_mine + cols_other, 0)
    frame_new = frame_factor * ring_sum(part, "x") / (col_chan * col_bins_new)
    return chan_new, bin_new, frame_new


def solution(mesh):
    split_mesh = Mesh(mesh.devices.reshape([SIZES[axis] for axis in AXES]), AXES)
    frames = ("y", "z", "core")
    in_specs = (P(frames, "x", None), P("x", None), P(AXES, None), P(frames, None))
    out_specs = (P("x", None), P(AXES, None), P(frames, None))
    return jax.shard_map(shards, mesh=split_mesh, in_specs=in_specs, out_specs=out_specs, check_vma=False)
```

```python
import functools
import math

import jax
import jax.numpy as jnp
from jax import lax
from jax.experimental import pallas as pl
from jax.experimental.pallas import tpu as pltpu
from jax.sharding import Mesh, PartitionSpec as P

AXES = ("y", "z", "core", "x")
CHIPS = ("y", "z", "x")
PLANE = ("y", "z")
SIZES = {"y": 4, "z": 4, "core": 2, "x": 4}
F32 = jnp.float32
BF16 = jnp.bfloat16
NT = (((1,), (1,)), ((), ()))
NN = (((1,), (0,)), ((), ()))
HIGH = lax.Precision.HIGH
VMEM = pl.BlockSpec(memory_space=pltpu.VMEM)
TILE = 512
CHUNK = 256
WIDE = 512


def shift(value, axis, step):
    size = SIZES[axis]
    return lax.ppermute(value, axis, [(i, (i + step) % size) for i in range(size)])


def ring_sum(value, axis):
    total = value
    for step in range(1, SIZES[axis]):
        total = total + shift(value, axis, step)
    return total


def exchange(value, axes):
    return lax.all_to_all(value, axes, 0, 0, tiled=True)


def split(value):
    high = value.astype(BF16)
    return high, (value - high.astype(F32)).astype(BF16)


def triple(value, axis, order):
    high, low = split(value)
    parts = {"h": high, "l": low}
    return jnp.concatenate([parts[part] for part in order], axis)


def product(left, right, dims, precision=None):
    return lax.dot_general(left, right, dims, precision=precision, preferred_element_type=F32)


def khatri_of(frames, chans):
    return (frames[:, None, :] * chans[None, :, :]).reshape(-1, chans.shape[1])


def half_lanes(x_ref, rows, start, count, parity):
    lane = lax.broadcasted_iota(jnp.int32, (rows.size, 128), 1)
    lower = lane < 64
    keep = lower == (parity == 0)
    pieces = []
    for at in range(2 * start, 2 * (start + count), 256):
        first = x_ref[rows, at : at + 128]
        second = x_ref[rows, at + 128 : at + 256]
        straight = jnp.where(lower, first, second)
        crossed = pltpu.roll(jnp.where(lower, second, first), 64, 1)
        pieces.append(jnp.where(keep, straight, crossed))
    return jnp.concatenate(pieces, 1)


def ratio_of(x_ref, rows, start, parity, model):
    guess = pl.reciprocal(model, approx=True)
    inverse = guess * (2.0 - model * guess)
    return half_lanes(x_ref, rows, start, model.shape[1], parity) * inverse


def parity_of(mine):
    core = lax.axis_index("core")
    return core if mine else 1 - core


def row_sums(value):
    return jnp.sum(value.reshape(-1, 8, value.shape[1]), 0)


def project_kernel(over, mine, x_ref, frames_ref, chans_ref, bins_ref, *rest):
    before_ref = None
    if not mine:
        before_ref, rest = rest[0], rest[1:]
    out_ref, cols_ref, khatri_ref, total_ref = rest
    frames, chans = frames_ref[...], chans_ref[...]
    parity = parity_of(mine)
    khatri_ref[...] = khatri_of(frames, chans)
    count = bins_ref.shape[0]
    for start in range(0, count, TILE):
        bins = bins_ref[start : start + TILE, :]
        for at in range(0, x_ref.shape[0], CHUNK):
            rows = pl.ds(at, CHUNK)
            ratio = ratio_of(x_ref, rows, start, parity, product(khatri_ref[rows, :], bins, NT, HIGH))
            part = product(ratio, bins, NN, HIGH)
            total_ref[rows, :] = part if start == 0 else total_ref[rows, :] + part
    projected = total_ref[...].reshape(frames.shape[0], chans.shape[0], -1)
    if over == "frames":
        result = jnp.sum(projected * frames[:, None, :], 0)
    else:
        result = jnp.sum(projected * chans[None, :, :], 1)
    size = result.shape[0]
    if before_ref is not None:
        result = result + before_ref[:size, :]
    if over == "frames":
        result = jnp.concatenate([result, row_sums(frames)], 0)
    for at in range(0, out_ref.shape[0], result.shape[0]):
        out_ref[at : at + result.shape[0], :] = result
    cols_ref[...] = row_sums(bins_ref[...])


def spread_kernel(mine, x_ref, frames_ref, chans_ref, bins_ref, out_ref, khatri_ref, turned_ref):
    parity = parity_of(mine)
    khatri = khatri_of(frames_ref[...], chans_ref[...])
    khatri_ref[...] = triple(khatri, 1, "hlh")
    high, low = split(khatri.T)
    turned_ref[0] = high
    turned_ref[1] = low
    count = bins_ref.shape[0]
    for start in range(0, count, TILE):
        bins_right = triple(bins_ref[start : start + TILE, :], 1, "hhl")
        total = None
        for at in range(0, x_ref.shape[0], WIDE):
            rows = pl.ds(at, WIDE)
            model = product(khatri_ref[rows, :], bins_right, NT)
            ratio = ratio_of(x_ref, rows, start, parity, model)
            left = jnp.concatenate([turned_ref[0, :, rows], turned_ref[0, :, rows], turned_ref[1, :, rows]], 1)
            part = product(left, triple(ratio, 0, "hlh"), NN)
            total = part if total is None else total + part
        out_ref[start : start + TILE, :] = total.T


def call(kernel, out_shape, scratch, x, frames, chans, bins, *more, limit=8, name):
    rows, count, rank = x.shape[0], bins.shape[0], bins.shape[1]
    return pl.pallas_call(
        kernel,
        in_specs=[VMEM] * (4 + len(more)),
        out_specs=jax.tree.map(lambda _: VMEM, out_shape),
        out_shape=out_shape,
        scratch_shapes=scratch,
        compiler_params=pltpu.CompilerParams(vmem_limit_bytes=limit << 20),
        cost_estimate=pl.CostEstimate(
            flops=12 * rows * count * rank, bytes_accessed=4 * (rows + rank) * count, transcendentals=rows * count
        ),
        name=name,
    )(x, frames, chans, bins, *more)


def project(over, mine, x, frames, chans, bins, *before, count=1):
    rank = bins.shape[1]
    out_rows = count * (chans.shape[0] + 8 if over == "frames" else frames.shape[0])
    out_shape = (jax.ShapeDtypeStruct((out_rows, rank), F32), jax.ShapeDtypeStruct((8, rank), F32))
    scratch = [pltpu.VMEM((x.shape[0], rank), F32), pltpu.VMEM((x.shape[0], rank), F32)]
    kernel = functools.partial(project_kernel, over, mine)
    return call(kernel, out_shape, scratch, x, frames, chans, bins, *before, name="project")


def spread(mine, x, frames, chans, bins):
    rank = bins.shape[1]
    out_shape = jax.ShapeDtypeStruct(bins.shape, F32)
    scratch = [pltpu.VMEM((x.shape[0], 3 * rank), BF16), pltpu.VMEM((2, rank, x.shape[0]), BF16)]
    return call(functools.partial(spread_kernel, mine), out_shape, scratch, x, frames, chans, bins, limit=16, name="spread")


LONG = pl.CostEstimate(flops=30_000_000_000, bytes_accessed=0, transcendentals=0)


def copies_kernel(rows_ref, out_ref):
    rows = rows_ref[...]
    for at in range(0, out_ref.shape[0], rows.shape[0]):
        out_ref[at : at + rows.shape[0], :] = rows


def copies(rows, count):
    return pl.pallas_call(
        copies_kernel,
        in_specs=[VMEM],
        out_specs=VMEM,
        out_shape=jax.ShapeDtypeStruct((rows.shape[0] * count, rows.shape[1]), F32),
        compiler_params=pltpu.CompilerParams(vmem_limit_bytes=8 << 20),
        cost_estimate=LONG,
        name="copies",
    )(rows)


def collect_kernel(pieces_ref, chans_ref, out_ref):
    size = out_ref.shape[0] - 8
    total = pieces_ref[:size, :]
    for at in range(size, pieces_ref.shape[0], size):
        total = total + pieces_ref[at : at + size, :]
    out_ref[:size, :] = total
    out_ref[size:, :] = jnp.broadcast_to(jnp.sum(chans_ref[...], 0, keepdims=True), (8, out_ref.shape[1]))


def collect(pieces, chans, line_count):
    return pl.pallas_call(
        collect_kernel,
        in_specs=[VMEM] * 2,
        out_specs=VMEM,
        out_shape=jax.ShapeDtypeStruct((line_count + 8, pieces.shape[1]), F32),
        compiler_params=pltpu.CompilerParams(vmem_limit_bytes=8 << 20),
        name="collect",
    )(pieces, chans)


def fold_kernel(pieces_ref, out_ref):
    size = out_ref.shape[0]
    total = pieces_ref[:size, :]
    for at in range(size, pieces_ref.shape[0], size):
        total = total + pieces_ref[at : at + size, :]
    out_ref[...] = total


def fold(pieces, size):
    return pl.pallas_call(
        fold_kernel,
        in_specs=[VMEM],
        out_specs=VMEM,
        out_shape=jax.ShapeDtypeStruct((size, pieces.shape[1]), F32),
        compiler_params=pltpu.CompilerParams(vmem_limit_bytes=8 << 20),
        name="fold",
    )(pieces)


def renew_kernel(sums_ref, bins_ref, col_frames_ref, line_ref, col_chan_ref):
    line_count = bins_ref.shape[0] // (SIZES["y"] * SIZES["z"])
    place = lax.axis_index("y") * SIZES["z"] + lax.axis_index("z")
    col_chan = sums_ref[line_count : line_count + 1, :]
    scale = 1.0 / (col_chan * col_frames_ref[...])
    old = bins_ref[pl.ds(pl.multiple_of(place * line_count, line_count), line_count), :]
    new = old * sums_ref[:line_count, :] * scale
    for at in range(0, line_ref.shape[0], line_count):
        line_ref[at : at + line_count, :] = new
    col_chan_ref[...] = col_chan


def renew(sums, bins, col_frames):
    shapes = (bins.shape, (1, bins.shape[1]))
    return pl.pallas_call(
        renew_kernel,
        in_specs=[VMEM] * 3,
        out_specs=[VMEM] * 2,
        out_shape=[jax.ShapeDtypeStruct(shape, F32) for shape in shapes],
        compiler_params=pltpu.CompilerParams(vmem_limit_bytes=8 << 20),
        cost_estimate=LONG,
        name="renew",
    )(sums, bins, col_frames)


def own_kernel(bins_ref, after_ref, out_ref):
    del after_ref
    place = lax.axis_index("y") * SIZES["z"] + lax.axis_index("z")
    start = (place * SIZES["x"] + lax.axis_index("x")) * out_ref.shape[0]
    out_ref[...] = bins_ref[pl.ds(pl.multiple_of(start, out_ref.shape[0]), out_ref.shape[0]), :]


def own_rows(bins, after, own_count):
    return pl.pallas_call(
        own_kernel,
        in_specs=[VMEM] * 2,
        out_specs=VMEM,
        out_shape=jax.ShapeDtypeStruct((own_count, bins.shape[1]), F32),
        compiler_params=pltpu.CompilerParams(vmem_limit_bytes=8 << 20),
        name="own_rows",
    )(bins, after)


def shards(spectra, chan_factor, bin_factor, frame_factor):
    frame_count, chan_count, bin_count = spectra.shape
    rank_count = chan_factor.shape[1]
    own_count = bin_factor.shape[0]
    x = spectra.reshape(frame_count * chan_count, bin_count)

    bins_mine = exchange(copies(bin_factor, math.prod(SIZES[axis] for axis in CHIPS)), CHIPS)
    bins_other = shift(bins_mine, "core", 1)
    sums, cols_mine = project("frames", True, x, frame_factor, chan_factor, bins_mine)
    places = SIZES["y"] * SIZES["z"]
    sums, cols_other = project("frames", False, x, frame_factor, chan_factor, bins_other, sums, count=places)
    col_bins = jnp.sum(cols_mine + cols_other, 0)
    sums = ring_sum(fold(exchange(sums, PLANE), sums.shape[0] // places), "core")
    col_frames = jnp.sum(sums[chan_count:], 0, keepdims=True)
    chan_new = chan_factor * sums[:chan_count] / (col_bins * col_frames)

    part_other = spread(False, x, frame_factor, chan_new, bins_other)
    arrived = shift(part_other, "core", 1)
    part_mine = spread(True, x, frame_factor, chan_new, bins_mine)
    line_count = own_count * SIZES["x"]
    pieces = exchange(part_mine + arrived, PLANE)
    sums = ring_sum(collect(pieces, chan_new, line_count), "x")
    line_bins, col_chan = renew(sums, bins_mine, col_frames)

    bins_mine = exchange(line_bins, PLANE)
    bins_other = shift(bins_mine, "core", 1)
    part, cols_mine = project("chans", True, x, frame_factor, chan_new, bins_mine)
    part, cols_other = project("chans", False, x, frame_factor, chan_new, bins_other, part)
    bin_new = own_rows(bins_mine, cols_other, own_count)
    col_bins_new = jnp.sum(cols_mine + cols_other, 0)
    frame_new = frame_factor * ring_sum(part, "x") / (col_chan * col_bins_new)
    return chan_new, bin_new, frame_new


def solution(mesh):
    split_mesh = Mesh(mesh.devices.reshape([SIZES[axis] for axis in AXES]), AXES)
    frames = ("y", "z", "core")
    in_specs = (P(frames, "x", None), P("x", None), P(AXES, None), P(frames, None))
    out_specs = (P("x", None), P(AXES, None), P(frames, None))
    return jax.shard_map(shards, mesh=split_mesh, in_specs=in_specs, out_specs=out_specs, check_vma=False)
```

```python
import functools
import math

import jax
import jax.numpy as jnp
from jax import lax
from jax.experimental import pallas as pl
from jax.experimental.pallas import tpu as pltpu
from jax.sharding import Mesh, PartitionSpec as P

AXES = ("y", "z", "core", "x")
CHIPS = ("y", "z", "x")
PLANE = ("y", "z")
SIZES = {"y": 4, "z": 4, "core": 2, "x": 4}
F32 = jnp.float32
BF16 = jnp.bfloat16
NT = (((1,), (1,)), ((), ()))
NN = (((1,), (0,)), ((), ()))
HIGH = lax.Precision.HIGH
VMEM = pl.BlockSpec(memory_space=pltpu.VMEM)
TILE = 512
CHUNK = 256
WIDE = 512
BROAD = 1024


def shift(value, axis, step):
    size = SIZES[axis]
    return lax.ppermute(value, axis, [(i, (i + step) % size) for i in range(size)])


def ring_sum(value, axis):
    total = value
    for step in range(1, SIZES[axis]):
        total = total + shift(value, axis, step)
    return total


def exchange(value, axes):
    return lax.all_to_all(value, axes, 0, 0, tiled=True)


def split(value):
    high = value.astype(BF16)
    return high, (value - high.astype(F32)).astype(BF16)


def triple(value, axis, order):
    high, low = split(value)
    parts = {"h": high, "l": low}
    return jnp.concatenate([parts[part] for part in order], axis)


def product(left, right, dims, precision=None):
    return lax.dot_general(left, right, dims, precision=precision, preferred_element_type=F32)


def khatri_of(frames, chans):
    return (frames[:, None, :] * chans[None, :, :]).reshape(-1, chans.shape[1])


def half_lanes(x_ref, rows, start, count, parity):
    lane = lax.broadcasted_iota(jnp.int32, (rows.size, 128), 1)
    lower = lane < 64
    keep = lower == (parity == 0)
    pieces = []
    for at in range(2 * start, 2 * (start + count), 256):
        first = x_ref[rows, at : at + 128]
        second = x_ref[rows, at + 128 : at + 256]
        straight = jnp.where(lower, first, second)
        crossed = pltpu.roll(jnp.where(lower, second, first), 64, 1)
        pieces.append(jnp.where(keep, straight, crossed))
    return jnp.concatenate(pieces, 1)


def ratio_of(x_ref, rows, start, parity, model):
    guess = pl.reciprocal(model, approx=True)
    inverse = guess * (2.0 - model * guess)
    return half_lanes(x_ref, rows, start, model.shape[1], parity) * inverse


def parity_of(mine):
    core = lax.axis_index("core")
    return core if mine else 1 - core


def row_sums(value):
    return jnp.sum(value.reshape(-1, 8, value.shape[1]), 0)


def project_kernel(over, mine, x_ref, frames_ref, chans_ref, bins_ref, *rest):
    before_ref = None
    if not mine:
        before_ref, rest = rest[0], rest[1:]
    out_ref, cols_ref, khatri_ref, total_ref = rest
    frames, chans = frames_ref[...], chans_ref[...]
    parity = parity_of(mine)
    khatri_ref[...] = khatri_of(frames, chans)
    count = bins_ref.shape[0]
    for start in range(0, count, TILE):
        bins = bins_ref[start : start + TILE, :]
        for at in range(0, x_ref.shape[0], CHUNK):
            rows = pl.ds(at, CHUNK)
            ratio = ratio_of(x_ref, rows, start, parity, product(khatri_ref[rows, :], bins, NT, HIGH))
            part = product(ratio, bins, NN, HIGH)
            total_ref[rows, :] = part if start == 0 else total_ref[rows, :] + part
    projected = total_ref[...].reshape(frames.shape[0], chans.shape[0], -1)
    if over == "frames":
        result = jnp.sum(projected * frames[:, None, :], 0)
        result = jnp.concatenate([result[:, :128], result[:, 128:]], 0)
    else:
        result = jnp.sum(projected * chans[None, :, :], 1)
    size = result.shape[0]
    if before_ref is not None:
        result = result + before_ref[:size, :]
    if over == "frames":
        cols = jnp.broadcast_to(jnp.sum(frames, 0, keepdims=True), (8, frames.shape[1]))
        row = lax.broadcasted_iota(jnp.int32, (8, 128), 0)
        cols = jnp.where(row == 0, cols[:, :128], jnp.where(row == 1, cols[:, 128:], 0.0))
        result = jnp.concatenate([result, cols], 0)
    for at in range(0, out_ref.shape[0], result.shape[0]):
        out_ref[at : at + result.shape[0], :] = result
    cols_ref[...] = row_sums(bins_ref[...])


def spread_kernel(mine, x_ref, frames_ref, chans_ref, bins_ref, out_ref, khatri_ref, turned_ref):
    parity = parity_of(mine)
    khatri = khatri_of(frames_ref[...], chans_ref[...])
    khatri_ref[...] = triple(khatri, 1, "hlh")
    high, low = split(khatri.T)
    turned_ref[0] = high
    turned_ref[1] = low
    count = bins_ref.shape[0]
    for start in range(0, count, BROAD):
        bins_right = triple(bins_ref[start : start + BROAD, :], 1, "hhl")
        total = None
        for at in range(0, x_ref.shape[0], WIDE):
            rows = pl.ds(at, WIDE)
            model = product(khatri_ref[rows, :], bins_right, NT)
            ratio = ratio_of(x_ref, rows, start, parity, model)
            left = jnp.concatenate([turned_ref[0, :, rows], turned_ref[0, :, rows], turned_ref[1, :, rows]], 1)
            part = product(left, triple(ratio, 0, "hlh"), NN)
            total = part if total is None else total + part
        out_ref[start : start + BROAD, :] = total.T


def call(kernel, out_shape, scratch, x, frames, chans, bins, *more, limit=8, name):
    rows, count, rank = x.shape[0], bins.shape[0], bins.shape[1]
    return pl.pallas_call(
        kernel,
        in_specs=[VMEM] * (4 + len(more)),
        out_specs=jax.tree.map(lambda _: VMEM, out_shape),
        out_shape=out_shape,
        scratch_shapes=scratch,
        compiler_params=pltpu.CompilerParams(vmem_limit_bytes=limit << 20),
        cost_estimate=pl.CostEstimate(
            flops=12 * rows * count * rank, bytes_accessed=4 * (rows + rank) * count, transcendentals=rows * count
        ),
        name=name,
    )(x, frames, chans, bins, *more)


def project(over, mine, x, frames, chans, bins, *before, count=1):
    rank = bins.shape[1]
    rows = (count * (2 * chans.shape[0] + 8), rank // 2) if over == "frames" else (frames.shape[0], rank)
    out_shape = (jax.ShapeDtypeStruct(rows, F32), jax.ShapeDtypeStruct((8, rank), F32))
    scratch = [pltpu.VMEM((x.shape[0], rank), F32), pltpu.VMEM((x.shape[0], rank), F32)]
    kernel = functools.partial(project_kernel, over, mine)
    return call(kernel, out_shape, scratch, x, frames, chans, bins, *before, name="project")


def spread(mine, x, frames, chans, bins):
    rank = bins.shape[1]
    out_shape = jax.ShapeDtypeStruct(bins.shape, F32)
    scratch = [pltpu.VMEM((x.shape[0], 3 * rank), BF16), pltpu.VMEM((2, rank, x.shape[0]), BF16)]
    return call(functools.partial(spread_kernel, mine), out_shape, scratch, x, frames, chans, bins, limit=24, name="spread")


LONG = pl.CostEstimate(flops=30_000_000_000, bytes_accessed=0, transcendentals=0)


def copies_kernel(rows_ref, out_ref):
    rows = rows_ref[...]
    for at in range(0, out_ref.shape[0], rows.shape[0]):
        out_ref[at : at + rows.shape[0], :] = rows


def copies(rows, count):
    return pl.pallas_call(
        copies_kernel,
        in_specs=[VMEM],
        out_specs=VMEM,
        out_shape=jax.ShapeDtypeStruct((rows.shape[0] * count, rows.shape[1]), F32),
        compiler_params=pltpu.CompilerParams(vmem_limit_bytes=8 << 20),
        cost_estimate=LONG,
        name="copies",
    )(rows)


def collect_kernel(pieces_ref, chans_ref, out_ref):
    size = out_ref.shape[0] - 8
    total = pieces_ref[:size, :]
    for at in range(size, pieces_ref.shape[0], size):
        total = total + pieces_ref[at : at + size, :]
    out_ref[:size, :] = total
    out_ref[size:, :] = jnp.broadcast_to(jnp.sum(chans_ref[...], 0, keepdims=True), (8, out_ref.shape[1]))


def collect(pieces, chans, line_count):
    return pl.pallas_call(
        collect_kernel,
        in_specs=[VMEM] * 2,
        out_specs=VMEM,
        out_shape=jax.ShapeDtypeStruct((line_count + 8, pieces.shape[1]), F32),
        compiler_params=pltpu.CompilerParams(vmem_limit_bytes=8 << 20),
        name="collect",
    )(pieces, chans)


def fold_kernel(pieces_ref, out_ref):
    size = out_ref.shape[0]
    total = pieces_ref[:size, :]
    for at in range(size, pieces_ref.shape[0], size):
        total = total + pieces_ref[at : at + size, :]
    out_ref[...] = total


def fold(pieces, size):
    return pl.pallas_call(
        fold_kernel,
        in_specs=[VMEM],
        out_specs=VMEM,
        out_shape=jax.ShapeDtypeStruct((size, pieces.shape[1]), F32),
        compiler_params=pltpu.CompilerParams(vmem_limit_bytes=8 << 20),
        name="fold",
    )(pieces)


def renew_kernel(sums_ref, bins_ref, col_frames_ref, line_ref, col_chan_ref):
    line_count = bins_ref.shape[0] // (SIZES["y"] * SIZES["z"])
    place = lax.axis_index("y") * SIZES["z"] + lax.axis_index("z")
    col_chan = sums_ref[line_count : line_count + 1, :]
    scale = 1.0 / (col_chan * col_frames_ref[...])
    old = bins_ref[pl.ds(pl.multiple_of(place * line_count, line_count), line_count), :]
    new = old * sums_ref[:line_count, :] * scale
    for at in range(0, line_ref.shape[0], line_count):
        line_ref[at : at + line_count, :] = new
    col_chan_ref[...] = col_chan


def renew(sums, bins, col_frames):
    shapes = (bins.shape, (1, bins.shape[1]))
    return pl.pallas_call(
        renew_kernel,
        in_specs=[VMEM] * 3,
        out_specs=[VMEM] * 2,
        out_shape=[jax.ShapeDtypeStruct(shape, F32) for shape in shapes],
        compiler_params=pltpu.CompilerParams(vmem_limit_bytes=8 << 20),
        cost_estimate=LONG,
        name="renew",
    )(sums, bins, col_frames)


def own_kernel(bins_ref, after_ref, out_ref):
    del after_ref
    place = lax.axis_index("y") * SIZES["z"] + lax.axis_index("z")
    start = (place * SIZES["x"] + lax.axis_index("x")) * out_ref.shape[0]
    out_ref[...] = bins_ref[pl.ds(pl.multiple_of(start, out_ref.shape[0]), out_ref.shape[0]), :]


def own_rows(bins, after, own_count):
    return pl.pallas_call(
        own_kernel,
        in_specs=[VMEM] * 2,
        out_specs=VMEM,
        out_shape=jax.ShapeDtypeStruct((own_count, bins.shape[1]), F32),
        compiler_params=pltpu.CompilerParams(vmem_limit_bytes=8 << 20),
        name="own_rows",
    )(bins, after)


def shards(spectra, chan_factor, bin_factor, frame_factor):
    frame_count, chan_count, bin_count = spectra.shape
    rank_count = chan_factor.shape[1]
    own_count = bin_factor.shape[0]
    x = spectra.reshape(frame_count * chan_count, bin_count)

    bins_mine = exchange(copies(bin_factor, math.prod(SIZES[axis] for axis in CHIPS)), CHIPS)
    bins_other = shift(bins_mine, "core", 1)
    sums, cols_mine = project("frames", True, x, frame_factor, chan_factor, bins_mine)
    places = SIZES["y"] * SIZES["z"]
    sums, cols_other = project("frames", False, x, frame_factor, chan_factor, bins_other, sums, count=places)
    col_bins = jnp.sum(cols_mine + cols_other, 0)
    sums = ring_sum(fold(exchange(sums, PLANE), sums.shape[0] // places), "core")
    col_frames = jnp.concatenate([sums[2 * chan_count : 2 * chan_count + 1], sums[2 * chan_count + 1 : 2 * chan_count + 2]], 1)
    num_chan = jnp.concatenate([sums[:chan_count], sums[chan_count : 2 * chan_count]], 1)
    chan_new = chan_factor * num_chan / (col_bins * col_frames)

    part_other = spread(False, x, frame_factor, chan_new, bins_other)
    arrived = shift(part_other, "core", 1)
    part_mine = spread(True, x, frame_factor, chan_new, bins_mine)
    line_count = own_count * SIZES["x"]
    pieces = exchange(part_mine + arrived, PLANE)
    sums = ring_sum(collect(pieces, chan_new, line_count), "x")
    line_bins, col_chan = renew(sums, bins_mine, col_frames)

    bins_mine = exchange(line_bins, PLANE)
    bins_other = shift(bins_mine, "core", 1)
    part, cols_mine = project("chans", True, x, frame_factor, chan_new, bins_mine)
    part, cols_other = project("chans", False, x, frame_factor, chan_new, bins_other, part)
    bin_new = own_rows(bins_mine, cols_other, own_count)
    col_bins_new = jnp.sum(cols_mine + cols_other, 0)
    frame_new = frame_factor * ring_sum(part, "x") / (col_chan * col_bins_new)
    return chan_new, bin_new, frame_new


def solution(mesh):
    split_mesh = Mesh(mesh.devices.reshape([SIZES[axis] for axis in AXES]), AXES)
    frames = ("y", "z", "core")
    in_specs = (P(frames, "x", None), P("x", None), P(AXES, None), P(frames, None))
    out_specs = (P("x", None), P(AXES, None), P(frames, None))
    return jax.shard_map(shards, mesh=split_mesh, in_specs=in_specs, out_specs=out_specs, check_vma=False)
```

```python
import functools
import math

import jax
import jax.numpy as jnp
from jax import lax
from jax.experimental import pallas as pl
from jax.experimental.pallas import tpu as pltpu
from jax.sharding import Mesh, PartitionSpec as P

AXES = ("y", "z", "core", "x")
CHIPS = ("y", "z", "x")
PLANE = ("y", "z")
SIZES = {"y": 4, "z": 4, "core": 2, "x": 4}
F32 = jnp.float32
BF16 = jnp.bfloat16
NT = (((1,), (1,)), ((), ()))
NN = (((1,), (0,)), ((), ()))
HIGH = lax.Precision.HIGH
VMEM = pl.BlockSpec(memory_space=pltpu.VMEM)
TILE = 512
CHUNK = 256
WIDE = 512
BROAD = 1024


def shift(value, axis, step):
    size = SIZES[axis]
    return lax.ppermute(value, axis, [(i, (i + step) % size) for i in range(size)])


def ring_sum(value, axis):
    size = SIZES[axis]
    steps = sorted(range(1, size), key=lambda step: -min(step, size - step))
    return value + sum(shift(value, axis, step) for step in steps)


def exchange(value, axes):
    return lax.all_to_all(value, axes, 0, 0, tiled=True)


def split(value):
    high = value.astype(BF16)
    return high, (value - high.astype(F32)).astype(BF16)


def triple(value, axis, order):
    high, low = split(value)
    parts = {"h": high, "l": low}
    return jnp.concatenate([parts[part] for part in order], axis)


def product(left, right, dims, precision=None):
    return lax.dot_general(left, right, dims, precision=precision, preferred_element_type=F32)


def khatri_of(frames, chans):
    return (frames[:, None, :] * chans[None, :, :]).reshape(-1, chans.shape[1])


def half_lanes(x_ref, rows, start, count, parity):
    lane = lax.broadcasted_iota(jnp.int32, (rows.size, 128), 1)
    lower = lane < 64
    keep = lower == (parity == 0)
    pieces = []
    for at in range(2 * start, 2 * (start + count), 256):
        first = x_ref[rows, at : at + 128]
        second = x_ref[rows, at + 128 : at + 256]
        straight = jnp.where(lower, first, second)
        crossed = pltpu.roll(jnp.where(lower, second, first), 64, 1)
        pieces.append(jnp.where(keep, straight, crossed))
    return jnp.concatenate(pieces, 1)


def ratio_of(x_ref, rows, start, parity, model):
    guess = pl.reciprocal(model, approx=True)
    inverse = guess * (2.0 - model * guess)
    return half_lanes(x_ref, rows, start, model.shape[1], parity) * inverse


def parity_of(mine):
    core = lax.axis_index("core")
    return core if mine else 1 - core


def row_sums(value):
    return jnp.sum(value.reshape(-1, 8, value.shape[1]), 0)


def project_kernel(over, mine, x_ref, frames_ref, chans_ref, bins_ref, *rest):
    before_ref = None
    if not mine:
        before_ref, rest = rest[0], rest[1:]
    out_ref, cols_ref, khatri_ref, total_ref = rest
    frames, chans = frames_ref[...], chans_ref[...]
    parity = parity_of(mine)
    khatri_ref[...] = khatri_of(frames, chans)
    count = bins_ref.shape[0]
    for start in range(0, count, TILE):
        bins = bins_ref[start : start + TILE, :]
        for at in range(0, x_ref.shape[0], CHUNK):
            rows = pl.ds(at, CHUNK)
            ratio = ratio_of(x_ref, rows, start, parity, product(khatri_ref[rows, :], bins, NT, HIGH))
            part = product(ratio, bins, NN, HIGH)
            total_ref[rows, :] = part if start == 0 else total_ref[rows, :] + part
    projected = total_ref[...].reshape(frames.shape[0], chans.shape[0], -1)
    if over == "frames":
        result = jnp.sum(projected * frames[:, None, :], 0)
        result = jnp.concatenate([result[:, :128], result[:, 128:]], 0)
    else:
        result = jnp.sum(projected * chans[None, :, :], 1)
    size = result.shape[0]
    if before_ref is not None:
        result = result + before_ref[:size, :]
    if over == "frames":
        cols = jnp.broadcast_to(jnp.sum(frames, 0, keepdims=True), (8, frames.shape[1]))
        row = lax.broadcasted_iota(jnp.int32, (8, 128), 0)
        cols = jnp.where(row == 0, cols[:, :128], jnp.where(row == 1, cols[:, 128:], 0.0))
        result = jnp.concatenate([result, cols], 0)
    for at in range(0, out_ref.shape[0], result.shape[0]):
        out_ref[at : at + result.shape[0], :] = result
    cols_ref[...] = row_sums(bins_ref[...])


def spread_kernel(mine, x_ref, frames_ref, chans_ref, bins_ref, out_ref, khatri_ref, turned_ref):
    parity = parity_of(mine)
    khatri = khatri_of(frames_ref[...], chans_ref[...])
    khatri_ref[...] = triple(khatri, 1, "hlh")
    high, low = split(khatri.T)
    turned_ref[0] = high
    turned_ref[1] = low
    count = bins_ref.shape[0]
    for start in range(0, count, BROAD):
        bins_right = triple(bins_ref[start : start + BROAD, :], 1, "hhl")
        total = None
        for at in range(0, x_ref.shape[0], WIDE):
            rows = pl.ds(at, WIDE)
            model = product(khatri_ref[rows, :], bins_right, NT)
            ratio = ratio_of(x_ref, rows, start, parity, model)
            left = jnp.concatenate([turned_ref[0, :, rows], turned_ref[0, :, rows], turned_ref[1, :, rows]], 1)
            part = product(left, triple(ratio, 0, "hlh"), NN)
            total = part if total is None else total + part
        out_ref[start : start + BROAD, :] = total.T


def call(kernel, out_shape, scratch, x, frames, chans, bins, *more, limit=8, name):
    rows, count, rank = x.shape[0], bins.shape[0], bins.shape[1]
    return pl.pallas_call(
        kernel,
        in_specs=[VMEM] * (4 + len(more)),
        out_specs=jax.tree.map(lambda _: VMEM, out_shape),
        out_shape=out_shape,
        scratch_shapes=scratch,
        compiler_params=pltpu.CompilerParams(vmem_limit_bytes=limit << 20),
        cost_estimate=pl.CostEstimate(
            flops=12 * rows * count * rank, bytes_accessed=4 * (rows + rank) * count, transcendentals=rows * count
        ),
        name=name,
    )(x, frames, chans, bins, *more)


def project(over, mine, x, frames, chans, bins, *before, count=1):
    rank = bins.shape[1]
    rows = (count * (2 * chans.shape[0] + 8), rank // 2) if over == "frames" else (frames.shape[0], rank)
    out_shape = (jax.ShapeDtypeStruct(rows, F32), jax.ShapeDtypeStruct((8, rank), F32))
    scratch = [pltpu.VMEM((x.shape[0], rank), F32), pltpu.VMEM((x.shape[0], rank), F32)]
    kernel = functools.partial(project_kernel, over, mine)
    return call(kernel, out_shape, scratch, x, frames, chans, bins, *before, name="project")


def spread(mine, x, frames, chans, bins):
    rank = bins.shape[1]
    out_shape = jax.ShapeDtypeStruct(bins.shape, F32)
    scratch = [pltpu.VMEM((x.shape[0], 3 * rank), BF16), pltpu.VMEM((2, rank, x.shape[0]), BF16)]
    return call(functools.partial(spread_kernel, mine), out_shape, scratch, x, frames, chans, bins, limit=24, name="spread")


LONG = pl.CostEstimate(flops=30_000_000_000, bytes_accessed=0, transcendentals=0)


def copies_kernel(rows_ref, out_ref):
    rows = rows_ref[...]
    for at in range(0, out_ref.shape[0], rows.shape[0]):
        out_ref[at : at + rows.shape[0], :] = rows


def copies(rows, count):
    return pl.pallas_call(
        copies_kernel,
        in_specs=[VMEM],
        out_specs=VMEM,
        out_shape=jax.ShapeDtypeStruct((rows.shape[0] * count, rows.shape[1]), F32),
        compiler_params=pltpu.CompilerParams(vmem_limit_bytes=8 << 20),
        cost_estimate=LONG,
        name="copies",
    )(rows)


def collect_kernel(pieces_ref, chans_ref, out_ref):
    size = out_ref.shape[0] - 8
    total = pieces_ref[:size, :]
    for at in range(size, pieces_ref.shape[0], size):
        total = total + pieces_ref[at : at + size, :]
    out_ref[:size, :] = total
    out_ref[size:, :] = jnp.broadcast_to(jnp.sum(chans_ref[...], 0, keepdims=True), (8, out_ref.shape[1]))


def collect(pieces, chans, line_count):
    return pl.pallas_call(
        collect_kernel,
        in_specs=[VMEM] * 2,
        out_specs=VMEM,
        out_shape=jax.ShapeDtypeStruct((line_count + 8, pieces.shape[1]), F32),
        compiler_params=pltpu.CompilerParams(vmem_limit_bytes=8 << 20),
        name="collect",
    )(pieces, chans)


def fold_kernel(pieces_ref, out_ref):
    size = out_ref.shape[0]
    total = pieces_ref[:size, :]
    for at in range(size, pieces_ref.shape[0], size):
        total = total + pieces_ref[at : at + size, :]
    out_ref[...] = total


def fold(pieces, size):
    return pl.pallas_call(
        fold_kernel,
        in_specs=[VMEM],
        out_specs=VMEM,
        out_shape=jax.ShapeDtypeStruct((size, pieces.shape[1]), F32),
        compiler_params=pltpu.CompilerParams(vmem_limit_bytes=8 << 20),
        name="fold",
    )(pieces)


def renew_kernel(sums_ref, bins_ref, col_frames_ref, line_ref, col_chan_ref):
    line_count = bins_ref.shape[0] // (SIZES["y"] * SIZES["z"])
    place = lax.axis_index("y") * SIZES["z"] + lax.axis_index("z")
    col_chan = sums_ref[line_count : line_count + 1, :]
    scale = 1.0 / (col_chan * col_frames_ref[...])
    old = bins_ref[pl.ds(pl.multiple_of(place * line_count, line_count), line_count), :]
    new = old * sums_ref[:line_count, :] * scale
    for at in range(0, line_ref.shape[0], line_count):
        line_ref[at : at + line_count, :] = new
    col_chan_ref[...] = col_chan


def renew(sums, bins, col_frames):
    shapes = (bins.shape, (1, bins.shape[1]))
    return pl.pallas_call(
        renew_kernel,
        in_specs=[VMEM] * 3,
        out_specs=[VMEM] * 2,
        out_shape=[jax.ShapeDtypeStruct(shape, F32) for shape in shapes],
        compiler_params=pltpu.CompilerParams(vmem_limit_bytes=8 << 20),
        cost_estimate=LONG,
        name="renew",
    )(sums, bins, col_frames)


def own_kernel(bins_ref, after_ref, out_ref):
    del after_ref
    place = lax.axis_index("y") * SIZES["z"] + lax.axis_index("z")
    start = (place * SIZES["x"] + lax.axis_index("x")) * out_ref.shape[0]
    out_ref[...] = bins_ref[pl.ds(pl.multiple_of(start, out_ref.shape[0]), out_ref.shape[0]), :]


def own_rows(bins, after, own_count):
    return pl.pallas_call(
        own_kernel,
        in_specs=[VMEM] * 2,
        out_specs=VMEM,
        out_shape=jax.ShapeDtypeStruct((own_count, bins.shape[1]), F32),
        compiler_params=pltpu.CompilerParams(vmem_limit_bytes=8 << 20),
        name="own_rows",
    )(bins, after)


def shards(spectra, chan_factor, bin_factor, frame_factor):
    frame_count, chan_count, bin_count = spectra.shape
    rank_count = chan_factor.shape[1]
    own_count = bin_factor.shape[0]
    x = spectra.reshape(frame_count * chan_count, bin_count)

    bins_mine = exchange(copies(bin_factor, math.prod(SIZES[axis] for axis in CHIPS)), CHIPS)
    bins_other = shift(bins_mine, "core", 1)
    sums, cols_mine = project("frames", True, x, frame_factor, chan_factor, bins_mine)
    places = SIZES["y"] * SIZES["z"]
    sums, cols_other = project("frames", False, x, frame_factor, chan_factor, bins_other, sums, count=places)
    col_bins = jnp.sum(cols_mine + cols_other, 0)
    sums = ring_sum(fold(exchange(sums, PLANE), sums.shape[0] // places), "core")
    col_frames = jnp.concatenate([sums[2 * chan_count : 2 * chan_count + 1], sums[2 * chan_count + 1 : 2 * chan_count + 2]], 1)
    num_chan = jnp.concatenate([sums[:chan_count], sums[chan_count : 2 * chan_count]], 1)
    chan_new = chan_factor * num_chan / (col_bins * col_frames)

    part_other = spread(False, x, frame_factor, chan_new, bins_other)
    arrived = shift(part_other, "core", 1)
    part_mine = spread(True, x, frame_factor, chan_new, bins_mine)
    line_count = own_count * SIZES["x"]
    pieces = exchange(part_mine + arrived, PLANE)
    sums = ring_sum(collect(pieces, chan_new, line_count), "x")
    line_bins, col_chan = renew(sums, bins_mine, col_frames)

    bins_mine = exchange(line_bins, PLANE)
    bins_other = shift(bins_mine, "core", 1)
    part, cols_mine = project("chans", True, x, frame_factor, chan_new, bins_mine)
    part, cols_other = project("chans", False, x, frame_factor, chan_new, bins_other, part)
    bin_new = own_rows(bins_mine, cols_other, own_count)
    col_bins_new = jnp.sum(cols_mine + cols_other, 0)
    frame_new = frame_factor * ring_sum(part, "x") / (col_chan * col_bins_new)
    return chan_new, bin_new, frame_new


def solution(mesh):
    split_mesh = Mesh(mesh.devices.reshape([SIZES[axis] for axis in AXES]), AXES)
    frames = ("y", "z", "core")
    in_specs = (P(frames, "x", None), P("x", None), P(AXES, None), P(frames, None))
    out_specs = (P("x", None), P(AXES, None), P(frames, None))
    return jax.shard_map(shards, mesh=split_mesh, in_specs=in_specs, out_specs=out_specs, check_vma=False)
```

```python
import functools
import math

import jax
import jax.numpy as jnp
from jax import lax
from jax.experimental import pallas as pl
from jax.experimental.pallas import tpu as pltpu
from jax.sharding import Mesh, PartitionSpec as P

AXES = ("y", "z", "core", "x")
CHIPS = ("y", "z", "x")
PLANE = ("y", "z")
SIZES = {"y": 4, "z": 4, "core": 2, "x": 4}
F32 = jnp.float32
BF16 = jnp.bfloat16
NT = (((1,), (1,)), ((), ()))
NN = (((1,), (0,)), ((), ()))
HIGH = lax.Precision.HIGH
VMEM = pl.BlockSpec(memory_space=pltpu.VMEM)
TILE = 512
CHUNK = 256
WIDE = 512
BROAD = 1024


def shift(value, axis, step):
    size = SIZES[axis]
    return lax.ppermute(value, axis, [(i, (i + step) % size) for i in range(size)])


def ring_sum(value, axis):
    size = SIZES[axis]
    steps = sorted(range(1, size), key=lambda step: -min(step, size - step))
    return value + sum(shift(value, axis, step) for step in steps)


def exchange(value, axes):
    return lax.all_to_all(value, axes, 0, 0, tiled=True)


def split(value):
    high = value.astype(BF16)
    return high, (value - high.astype(F32)).astype(BF16)


def triple(value, axis, order):
    high, low = split(value)
    parts = {"h": high, "l": low}
    return jnp.concatenate([parts[part] for part in order], axis)


def product(left, right, dims, precision=None):
    return lax.dot_general(left, right, dims, precision=precision, preferred_element_type=F32)


def khatri_of(frames, chans):
    return (frames[:, None, :] * chans[None, :, :]).reshape(-1, chans.shape[1])


def half_lanes(x_ref, rows, start, count, parity):
    lane = lax.broadcasted_iota(jnp.int32, (rows.size, 128), 1)
    lower = lane < 64
    keep = lower == (parity == 0)
    pieces = []
    for at in range(2 * start, 2 * (start + count), 256):
        first = x_ref[rows, at : at + 128]
        second = x_ref[rows, at + 128 : at + 256]
        straight = jnp.where(lower, first, second)
        crossed = pltpu.roll(jnp.where(lower, second, first), 64, 1)
        pieces.append(jnp.where(keep, straight, crossed))
    return jnp.concatenate(pieces, 1)


def ratio_of(x_ref, rows, start, parity, model):
    guess = pl.reciprocal(model, approx=True)
    inverse = guess * (2.0 - model * guess)
    return half_lanes(x_ref, rows, start, model.shape[1], parity) * inverse


def parity_of(mine):
    core = lax.axis_index("core")
    return core if mine else 1 - core


def row_sums(value):
    return jnp.sum(value.reshape(-1, 8, value.shape[1]), 0)


def project_kernel(over, mine, x_ref, frames_ref, chans_ref, bins_ref, *rest):
    before_ref = None
    if not mine:
        before_ref, rest = rest[0], rest[1:]
    out_ref, cols_ref, khatri_ref, total_ref = rest
    frames, chans = frames_ref[...], chans_ref[...]
    parity = parity_of(mine)
    khatri_ref[...] = khatri_of(frames, chans)
    count = bins_ref.shape[0]
    for start in range(0, count, TILE):
        bins = bins_ref[start : start + TILE, :]
        for at in range(0, x_ref.shape[0], CHUNK):
            rows = pl.ds(at, CHUNK)
            ratio = ratio_of(x_ref, rows, start, parity, product(khatri_ref[rows, :], bins, NT, HIGH))
            part = product(ratio, bins, NN, HIGH)
            total_ref[rows, :] = part if start == 0 else total_ref[rows, :] + part
    projected = total_ref[...].reshape(frames.shape[0], chans.shape[0], -1)
    if over == "frames":
        result = jnp.sum(projected * frames[:, None, :], 0)
        result = jnp.concatenate([result[:, :128], result[:, 128:]], 0)
    else:
        result = jnp.sum(projected * chans[None, :, :], 1)
    size = result.shape[0]
    if before_ref is not None:
        result = result + before_ref[:size, :]
    if over == "frames":
        cols = jnp.broadcast_to(jnp.sum(frames, 0, keepdims=True), (8, frames.shape[1]))
        row = lax.broadcasted_iota(jnp.int32, (8, 128), 0)
        cols = jnp.where(row == 0, cols[:, :128], jnp.where(row == 1, cols[:, 128:], 0.0))
        result = jnp.concatenate([result, cols], 0)
    for at in range(0, out_ref.shape[0], result.shape[0]):
        out_ref[at : at + result.shape[0], :] = result
    cols_ref[...] = row_sums(bins_ref[...])


def spread_kernel(mine, x_ref, frames_ref, chans_ref, bins_ref, out_ref, khatri_ref, turned_ref):
    parity = parity_of(mine)
    khatri = khatri_of(frames_ref[...], chans_ref[...])
    khatri_ref[...] = triple(khatri, 1, "hlh")
    high, low = split(khatri.T)
    turned_ref[0] = high
    turned_ref[1] = low
    count = bins_ref.shape[0]
    for start in range(0, count, BROAD):
        bins_right = triple(bins_ref[start : start + BROAD, :], 1, "hhl")
        total = None
        for at in range(0, x_ref.shape[0], WIDE):
            rows = pl.ds(at, WIDE)
            model = product(khatri_ref[rows, :], bins_right, NT)
            ratio = ratio_of(x_ref, rows, start, parity, model)
            left = jnp.concatenate([turned_ref[0, :, rows], turned_ref[0, :, rows], turned_ref[1, :, rows]], 1)
            part = product(left, triple(ratio, 0, "hlh"), NN)
            total = part if total is None else total + part
        out_ref[start : start + BROAD, :] = total.T


def call(kernel, out_shape, scratch, x, frames, chans, bins, *more, limit=8, name):
    rows, count, rank = x.shape[0], bins.shape[0], bins.shape[1]
    return pl.pallas_call(
        kernel,
        in_specs=[VMEM] * (4 + len(more)),
        out_specs=jax.tree.map(lambda _: VMEM, out_shape),
        out_shape=out_shape,
        scratch_shapes=scratch,
        compiler_params=pltpu.CompilerParams(vmem_limit_bytes=limit << 20),
        cost_estimate=pl.CostEstimate(
            flops=12 * rows * count * rank, bytes_accessed=4 * (rows + rank) * count, transcendentals=rows * count
        ),
        name=name,
    )(x, frames, chans, bins, *more)


def project(over, mine, x, frames, chans, bins, *before, count=1):
    rank = bins.shape[1]
    rows = (count * (2 * chans.shape[0] + 8), rank // 2) if over == "frames" else (frames.shape[0], rank)
    out_shape = (jax.ShapeDtypeStruct(rows, F32), jax.ShapeDtypeStruct((8, rank), F32))
    scratch = [pltpu.VMEM((x.shape[0], rank), F32), pltpu.VMEM((x.shape[0], rank), F32)]
    kernel = functools.partial(project_kernel, over, mine)
    return call(kernel, out_shape, scratch, x, frames, chans, bins, *before, name="project")


def spread(mine, x, frames, chans, bins):
    rank = bins.shape[1]
    out_shape = jax.ShapeDtypeStruct(bins.shape, F32)
    scratch = [pltpu.VMEM((x.shape[0], 3 * rank), BF16), pltpu.VMEM((2, rank, x.shape[0]), BF16)]
    return call(functools.partial(spread_kernel, mine), out_shape, scratch, x, frames, chans, bins, limit=24, name="spread")


LONG = pl.CostEstimate(flops=30_000_000_000, bytes_accessed=0, transcendentals=0)


def copies_kernel(rows_ref, out_ref):
    rows = rows_ref[...]
    for at in range(0, out_ref.shape[0], rows.shape[0]):
        out_ref[at : at + rows.shape[0], :] = rows


def copies(rows, count):
    return pl.pallas_call(
        copies_kernel,
        in_specs=[VMEM],
        out_specs=VMEM,
        out_shape=jax.ShapeDtypeStruct((rows.shape[0] * count, rows.shape[1]), F32),
        compiler_params=pltpu.CompilerParams(vmem_limit_bytes=8 << 20),
        cost_estimate=LONG,
        name="copies",
    )(rows)


def collect_kernel(pieces_ref, chans_ref, out_ref):
    size = (out_ref.shape[0] - 8) // 2
    total = pieces_ref[:size, :]
    for at in range(size, pieces_ref.shape[0], size):
        total = total + pieces_ref[at : at + size, :]
    out_ref[:size, :] = total[:, :128]
    out_ref[size : 2 * size, :] = total[:, 128:]
    cols = jnp.broadcast_to(jnp.sum(chans_ref[...], 0, keepdims=True), (8, total.shape[1]))
    row = lax.broadcasted_iota(jnp.int32, (8, 128), 0)
    out_ref[2 * size :, :] = jnp.where(row == 0, cols[:, :128], jnp.where(row == 1, cols[:, 128:], 0.0))


def collect(pieces, chans, line_count):
    return pl.pallas_call(
        collect_kernel,
        in_specs=[VMEM] * 2,
        out_specs=VMEM,
        out_shape=jax.ShapeDtypeStruct((2 * line_count + 8, pieces.shape[1] // 2), F32),
        compiler_params=pltpu.CompilerParams(vmem_limit_bytes=8 << 20),
        name="collect",
    )(pieces, chans)


def fold_kernel(pieces_ref, out_ref):
    size = out_ref.shape[0]
    total = pieces_ref[:size, :]
    for at in range(size, pieces_ref.shape[0], size):
        total = total + pieces_ref[at : at + size, :]
    out_ref[...] = total


def fold(pieces, size):
    return pl.pallas_call(
        fold_kernel,
        in_specs=[VMEM],
        out_specs=VMEM,
        out_shape=jax.ShapeDtypeStruct((size, pieces.shape[1]), F32),
        compiler_params=pltpu.CompilerParams(vmem_limit_bytes=8 << 20),
        name="fold",
    )(pieces)


def renew_kernel(sums_ref, bins_ref, col_frames_ref, line_ref, col_chan_ref):
    line_count = bins_ref.shape[0] // (SIZES["y"] * SIZES["z"])
    place = lax.axis_index("y") * SIZES["z"] + lax.axis_index("z")
    at = 2 * line_count
    col_chan = jnp.concatenate([sums_ref[at : at + 1, :], sums_ref[at + 1 : at + 2, :]], 1)
    num_bins = jnp.concatenate([sums_ref[:line_count, :], sums_ref[line_count:at, :]], 1)
    scale = 1.0 / (col_chan * col_frames_ref[...])
    old = bins_ref[pl.ds(pl.multiple_of(place * line_count, line_count), line_count), :]
    new = old * num_bins * scale
    for at in range(0, line_ref.shape[0], line_count):
        line_ref[at : at + line_count, :] = new
    col_chan_ref[...] = col_chan


def renew(sums, bins, col_frames):
    shapes = (bins.shape, (1, bins.shape[1]))
    return pl.pallas_call(
        renew_kernel,
        in_specs=[VMEM] * 3,
        out_specs=[VMEM] * 2,
        out_shape=[jax.ShapeDtypeStruct(shape, F32) for shape in shapes],
        compiler_params=pltpu.CompilerParams(vmem_limit_bytes=8 << 20),
        cost_estimate=LONG,
        name="renew",
    )(sums, bins, col_frames)


def own_kernel(bins_ref, after_ref, out_ref):
    del after_ref
    place = lax.axis_index("y") * SIZES["z"] + lax.axis_index("z")
    start = (place * SIZES["x"] + lax.axis_index("x")) * out_ref.shape[0]
    out_ref[...] = bins_ref[pl.ds(pl.multiple_of(start, out_ref.shape[0]), out_ref.shape[0]), :]


def own_rows(bins, after, own_count):
    return pl.pallas_call(
        own_kernel,
        in_specs=[VMEM] * 2,
        out_specs=VMEM,
        out_shape=jax.ShapeDtypeStruct((own_count, bins.shape[1]), F32),
        compiler_params=pltpu.CompilerParams(vmem_limit_bytes=8 << 20),
        name="own_rows",
    )(bins, after)


def shards(spectra, chan_factor, bin_factor, frame_factor):
    frame_count, chan_count, bin_count = spectra.shape
    rank_count = chan_factor.shape[1]
    own_count = bin_factor.shape[0]
    x = spectra.reshape(frame_count * chan_count, bin_count)

    bins_mine = exchange(copies(bin_factor, math.prod(SIZES[axis] for axis in CHIPS)), CHIPS)
    bins_other = shift(bins_mine, "core", 1)
    sums, cols_mine = project("frames", True, x, frame_factor, chan_factor, bins_mine)
    places = SIZES["y"] * SIZES["z"]
    sums, cols_other = project("frames", False, x, frame_factor, chan_factor, bins_other, sums, count=places)
    col_bins = jnp.sum(cols_mine + cols_other, 0)
    sums = ring_sum(fold(exchange(sums, PLANE), sums.shape[0] // places), "core")
    col_frames = jnp.concatenate([sums[2 * chan_count : 2 * chan_count + 1], sums[2 * chan_count + 1 : 2 * chan_count + 2]], 1)
    num_chan = jnp.concatenate([sums[:chan_count], sums[chan_count : 2 * chan_count]], 1)
    chan_new = chan_factor * num_chan / (col_bins * col_frames)

    part_other = spread(False, x, frame_factor, chan_new, bins_other)
    arrived = shift(part_other, "core", 1)
    part_mine = spread(True, x, frame_factor, chan_new, bins_mine)
    line_count = own_count * SIZES["x"]
    pieces = exchange(part_mine + arrived, PLANE)
    sums = ring_sum(collect(pieces, chan_new, line_count), "x")
    line_bins, col_chan = renew(sums, bins_mine, col_frames)

    bins_mine = exchange(line_bins, PLANE)
    bins_other = shift(bins_mine, "core", 1)
    part, cols_mine = project("chans", True, x, frame_factor, chan_new, bins_mine)
    part, cols_other = project("chans", False, x, frame_factor, chan_new, bins_other, part)
    bin_new = own_rows(bins_mine, cols_other, own_count)
    col_bins_new = jnp.sum(cols_mine + cols_other, 0)
    frame_new = frame_factor * ring_sum(part, "x") / (col_chan * col_bins_new)
    return chan_new, bin_new, frame_new


def solution(mesh):
    split_mesh = Mesh(mesh.devices.reshape([SIZES[axis] for axis in AXES]), AXES)
    frames = ("y", "z", "core")
    in_specs = (P(frames, "x", None), P("x", None), P(AXES, None), P(frames, None))
    out_specs = (P("x", None), P(AXES, None), P(frames, None))
    return jax.shard_map(shards, mesh=split_mesh, in_specs=in_specs, out_specs=out_specs, check_vma=False)
```
